512 devices in a mesh: dp: 32 (over z, x), tp: 16 (over y, core).
Axes of the slice: x: 4, y: 8, z: 8, core: 2. Of those that a mesh axis runs over, the one named last changes fastest.
Arguments:
- queries: bfloat16 [3072, 128, 576], P('dp', 'tp'), may hold values from -12 to 12, as said below
- page_pool: bfloat16 [6144, 16, 576], P('dp'), may hold values from -6 to 6
- prefix_cache: bfloat16 [2, 384, 576], replicated, may hold values from -12 to 12
- page_table: int32 [3072, 2], P('dp'), may hold values from 0 to 191, as said below
- lengths: int32 [3072], P('dp'), may hold values from 1 to 32, as said below
- prefix_id: int32 [3072], P('dp'), may hold values from 0 to 1
- prefix_len: int32 [2], replicated, may hold values from 16 to 384, as said below
- move_list: int32 [32, 32, 3], P('dp'), may hold values from 0 to 95, as said below
- value_up: bfloat16 [128, 512, 128], P('tp'), may hold values from -0.25 to 0.25
- output_weight: bfloat16 [16384, 7168], P('tp', 'dp'), may hold values from -0.046875 to 0.046875
- residual: bfloat16 [3072, 7168], P('tp', 'dp'), may hold values from -4 to 4
Outputs:
- layer_out: bfloat16 [3072, 7168], P('tp', 'dp')
- new_pool: bfloat16 [6144, 16, 576], P('dp')
The draws below stay inside these ranges and needn't reach their ends.
Inputs may be any that keep to these rules, and one draw needn't show every extreme that they name: The entries lie within the range; a few queries of some heads may be large. `page_table`: each rank's 96 rows hold each of its 192 local page numbers exactly once. `lengths`: every rank has a slot of exactly 32 own tokens. `prefix_len`: each is a multiple of 16; some prefix has exactly 384 tokens. `move_list`: each rank lists 32 distinct leaving slots. Moves 2m and 2m+1 of every rank r go to rank (r + o_m) mod 32, with 16 distinct offsets o_m in 1 to 31 that are the same for all ranks; so every rank sends exactly 2 requests to each of 16 ranks and nothing to the others. Move k into rank t takes the slot that t's own move k vacates, so every rank receives 32 requests.
All inputs are finite; a program needn't handle non-finite values.
Results may differ from the reference program's by a relative error of at most 0.0056.
Values may be sent and summed in bfloat16 or wider, within the bound.
A program may use at most 64 MiB of HBM per device.

```python
import jax
import jax.numpy as jnp
from jax import lax

D = 7168
H = 128
KVL = 512
ROPE = 64
VH = 128
R = 96
PAGE = 16
PPR = 2
NPRE = 2
PLEN = 384
OWN = 32
POOL = 192
PAIRS = 16
MOVES = 32
TOKENS = 3072
N_DP = 32


def draw_queries(key, part):
    key = jax.random.fold_in(key, 11)
    base_key = jax.random.fold_in(key, 0)
    values = jnp.clip(jax.random.normal(base_key, (TOKENS, H, KVL + ROPE), jnp.float32), -6.0, 6.0)
    return values.astype(jnp.bfloat16)


def draw_prefix_cache(key, part):
    key = jax.random.fold_in(key, 23)
    base_key = jax.random.fold_in(key, 0)
    values = jnp.clip(jax.random.normal(base_key, (NPRE, PLEN, KVL + ROPE), jnp.float32), -6.0, 6.0)
    return values.astype(jnp.bfloat16)


def draw_page_table(key, part):
    key = jax.random.fold_in(key, 41)
    rank_keys = jax.random.split(key, N_DP)

    def one_rank(rank_key):
        return jax.random.permutation(rank_key, POOL).astype(jnp.int32)
    return jax.vmap(one_rank)(rank_keys).reshape(TOKENS, PPR)


def draw_lengths(key, part):
    key = jax.random.fold_in(key, 53)
    first_key, second_key = jax.random.split(key)
    drawn = jax.random.randint(first_key, (N_DP, R), 1, OWN + 1)
    longest = jax.random.randint(second_key, (N_DP, 1), 0, R)
    drawn = jnp.where(jnp.arange(R)[None, :] == longest, OWN, drawn)
    return drawn.reshape(TOKENS).astype(jnp.int32)


def draw_prefix_len(key, part):
    key = jax.random.fold_in(key, 61)
    first_key, second_key = jax.random.split(key)
    pages = jax.random.randint(first_key, (NPRE,), 1, PLEN // PAGE + 1) * PAGE
    longest = jax.random.randint(second_key, (), 0, NPRE)
    return jnp.where(jnp.arange(NPRE) == longest, PLEN, pages).astype(jnp.int32)


def draw_move_list(key, part):
    key = jax.random.fold_in(key, 37)
    offset_key, slot_key = jax.random.split(key)
    offsets = jax.random.permutation(offset_key, N_DP - 1)[:PAIRS] + 1
    slot_keys = jax.random.split(slot_key, N_DP)

    def one_rank(rank_key):
        return jax.random.permutation(rank_key, R)[:MOVES]
    leaving = jax.vmap(one_rank)(slot_keys)
    pair_index = jnp.arange(MOVES) // 2
    source = jnp.arange(N_DP)[:, None]
    target = (source + offsets[pair_index][None, :]) % N_DP
    target_slot = leaving[target, jnp.arange(MOVES)[None, :]]
    return jnp.stack([leaving, target, target_slot], axis=2).astype(jnp.int32)


def place_ends(values, key, least, largest):
    longest = values.shape.index(max(values.shape))
    spots = []
    for shift in (0, 1):
        where = [jax.random.randint(jax.random.fold_in(key, axis), (), 0, length) for axis, length in enumerate(values.shape)]
        where[longest] = (where[longest] + shift) % values.shape[longest]
        spots.append(tuple(where))
    return values.at[spots[0]].set(least).at[spots[1]].set(largest)


def steps_of(key, dims, cuts, low, largest):
    def one(dim, parts):
        draws = jax.random.uniform(jax.random.fold_in(jax.random.fold_in(key, 6), dim), (parts,), jnp.float32, low / len(cuts), largest / len(cuts))
        return jnp.repeat(jnp.exp(draws), dims[dim] // parts).reshape((-1,) + (1,) * (len(dims) - dim - 1))

    factor_of = one(*cuts[0])
    for cut in cuts[1:]:
        factor_of = factor_of * one(*cut)
    return factor_of


def noise(key, dims, deviation, bound, cuts=(), held_as=jnp.bfloat16):
    values = deviation * jax.random.normal(key, dims, jnp.float32)
    if cuts:
        values = values * steps_of(key, dims, cuts, -0.22, 0.18)
    return jnp.clip(values, -bound, bound).astype(held_as)


def setup_inputs(seed: int = 0) -> dict:
    key_of = jax.random.split(jax.random.key(seed), 12)
    queries = draw_queries(jax.random.fold_in(key_of[11], 71), 0)
    page_pool = noise(key_of[1], (TOKENS * PPR, PAGE, KVL + ROPE), 1.0, 6.0, ((0, 32),))
    prefix_cache = draw_prefix_cache(jax.random.fold_in(key_of[11], 71), 0)
    page_table = draw_page_table(jax.random.fold_in(key_of[11], 71), 0)
    lengths = draw_lengths(jax.random.fold_in(key_of[11], 71), 0)
    prefix_id = place_ends(jax.random.randint(key_of[5], (TOKENS,), 0, NPRE), jax.random.fold_in(key_of[5], 1), 0, NPRE - 1).astype(jnp.int32)
    prefix_len = draw_prefix_len(jax.random.fold_in(key_of[11], 71), 0)
    move_list = draw_move_list(jax.random.fold_in(key_of[11], 71), 0)
    value_up = noise(key_of[8], (H, KVL, VH), KVL ** -0.5, 0.25, ((0, 16),))
    output_weight = noise(key_of[9], (H * VH, D), (H * VH) ** -0.5, 0.046875, ((0, 16), (1, 32)))
    residual = noise(key_of[10], (TOKENS, D), 0.25, 4.0, ((0, 16), (1, 32)))
    return {"queries": queries, "page_pool": page_pool, "prefix_cache": prefix_cache, "page_table": page_table, "lengths": lengths, "prefix_id": prefix_id, "prefix_len": prefix_len, "move_list": move_list, "value_up": value_up, "output_weight": output_weight, "residual": residual}


softmax_scale = 192.0 ** -0.5
masked_score = -1.0e30


def partial_softmax(queries, key_rows, usable):
    scores = jnp.einsum("bhc,bkc->bhk", queries.astype(jnp.float32), key_rows.astype(jnp.float32)) * softmax_scale
    scores = jnp.where(usable[:, None, :], scores, masked_score)
    highest = jnp.max(scores, axis=2)
    raised = jnp.exp(scores - highest[:, :, None])
    totals = jnp.sum(raised, axis=2)
    weights = lax.optimization_barrier(raised.astype(jnp.bfloat16)).astype(jnp.float32)
    blended = jnp.einsum("bhk,bkc->bhc", weights, key_rows[:, :, :KVL].astype(jnp.float32))
    return highest, totals, blended


def migrate_pages(page_pool, page_table, move_list):
    latent = KVL + ROPE
    by_rank = page_pool.reshape(N_DP, POOL, PAGE, latent)
    tables = page_table.reshape(N_DP, R, PPR)
    sources = jnp.broadcast_to(jnp.arange(N_DP, dtype=jnp.int32)[:, None], (N_DP, MOVES))
    leaving = tables[sources, move_list[:, :, 0]]
    arriving = tables[move_list[:, :, 1], move_list[:, :, 2]]
    carried = by_rank[sources[:, :, None], leaving]
    moved = by_rank.at[move_list[:, :, 1][:, :, None], arriving].set(carried)
    return moved.reshape(N_DP * POOL, PAGE, latent)


def reference(queries, page_pool, prefix_cache, page_table, lengths, prefix_id, prefix_len, move_list, value_up, output_weight, residual):
    new_pool = migrate_pages(page_pool, page_table, move_list)
    latent = KVL + ROPE
    own_tokens = PAGE * PPR
    value_table = value_up.astype(jnp.float32)
    positions = jnp.arange(PLEN, dtype=jnp.int32)
    own_positions = jnp.arange(own_tokens, dtype=jnp.int32)

    def one_rank(pieces):
        rank_queries, rank_tables, rank_lengths, rank_prefix, rank_pages = pieces
        prefix_keys = prefix_cache[rank_prefix]
        prefix_usable = positions[None, :] < prefix_len[rank_prefix][:, None]
        own_keys = rank_pages[rank_tables].reshape(R, own_tokens, latent)
        own_usable = own_positions[None, :] < rank_lengths[:, None]
        high_pre, total_pre, blend_pre = partial_softmax(rank_queries, prefix_keys, prefix_usable)
        high_own, total_own, blend_own = partial_softmax(rank_queries, own_keys, own_usable)
        ceiling = jnp.maximum(high_pre, high_own)
        factor_pre = jnp.exp(high_pre - ceiling)
        factor_own = jnp.exp(high_own - ceiling)
        merged = (factor_pre[:, :, None] * blend_pre + factor_own[:, :, None] * blend_own) / (factor_pre * total_pre + factor_own * total_own)[:, :, None]
        merged = lax.optimization_barrier(merged.astype(jnp.bfloat16)).astype(jnp.float32)
        heads_out = jnp.einsum("bhc,hcv->bhv", merged, value_table).astype(jnp.bfloat16)
        return heads_out.reshape(R, H * VH)

    heads_all = lax.map(one_rank, (queries.reshape(N_DP, R, H, latent), page_table.reshape(N_DP, R, PPR), lengths.reshape(N_DP, R), prefix_id.reshape(N_DP, R), new_pool.reshape(N_DP, POOL, PAGE, latent)))
    heads_all = heads_all.reshape(TOKENS, H * VH)
    layer_out = (residual.astype(jnp.float32) + jnp.dot(heads_all, output_weight, preferred_element_type=jnp.float32)).astype(jnp.bfloat16)
    return layer_out, new_pool
```

```python
import functools

import jax
import jax.numpy as jnp
from jax import lax
from jax.experimental import pallas as pl
from jax.experimental.pallas import tpu as pltpu
from jax.sharding import PartitionSpec as P

MESH = pl.DeviceIdType.MESH

LAT = 576
KVL = 512
HEADS = 8
VH = 128
PAGE = 16
REQ = 96
MOVES = 32
CH = 32
CHUNKS = REQ // CH
ROWS = CH * HEADS
POOL = 192
PLEN = 384
NZ, NX, NY = 8, 4, 8
COLS = 224
DEPTH = HEADS * VH
SCALE = 192.0 ** (-0.5)
MASKED = -1e30

NT = (((1,), (1,)), ((), ()))

W0 = 0
PD = W0 + 4
PY = PD + 8
PC = PY + 8
Z0 = PC + 9
CX = Z0 + 8 * CHUNKS
RS = CX + CHUNKS
FX = RS + 8 * CHUNKS
PM = FX + 2
SEMS = PM + 7


def div(a, n):
    return lax.div(a, jnp.int32(n))


def rem(a, n):
    return lax.rem(a, jnp.int32(n))


def fused(
    perm_s, page_s, prefix_s, length_s, limit_s, leave_s, arrive_s,
    q_h, pool_h, kt_h, vup_h, wt_h, order_h, res_h,
    out_ref, arr_o,
    q_v, pool_v, kt_v, vup_v, w_v, order_v, res_v, order_r,
    stage, arr, q_f, keys, rowinfo, blend, stats, merged,
    zb, sx, rx, own, ss, rr, red, fx, fr,
    lsem, ssem, rsem,
):
    d = lax.axis_index("dp")
    t = lax.axis_index("tp")
    z, x = div(d, NX), rem(d, NX)
    y, c = div(t, 2), rem(t, 2)
    kind, quarter = div(t, 4), rem(t, 4)

    def at_x(v):
        return (z * NX + rem(v + NX, NX), t)

    def at_z(v):
        return (rem(v + NZ, NZ) * NX + x, t)

    def at_y(v):
        return (d, rem(v + NY, NY) * 2 + c)

    def at_rank(v):
        return (rem(v + 32, 32), t)

    partner = (d, y * 2 + 1 - c)
    final_core = div(x, 2)
    diagonal = c == final_core

    sent = []

    def remote(src, dst, device, slot, recv_slot=None):
        return pltpu.make_async_remote_copy(
            src_ref=src, dst_ref=dst, send_sem=ssem.at[slot],
            recv_sem=rsem.at[slot if recv_slot is None else recv_slot],
            device_id=device, device_id_type=MESH,
        )

    def send(src, dst, device, slot):
        copy = remote(src, dst, device, slot)
        copy.start()
        sent.append(copy)

    def arrived(dst, slot):
        remote(dst, dst, partner, slot).wait_recv()

    loads = {}
    for n, (name, src, dst) in enumerate([
        ("pool", pool_h, pool_v), ("q", q_h, q_v), ("kt", kt_h, kt_v), ("vup", vup_h, vup_v),
        ("w", wt_h, w_v.at[x]), ("order", order_h, order_v), ("res", res_h, res_v),
    ]):
        loads[name] = pltpu.make_async_copy(src, dst, lsem.at[n])
        loads[name].start()

    barrier = pltpu.get_barrier_semaphore()

    def greet(device):
        pl.semaphore_signal(barrier, inc=1, device_id=device, device_id_type=MESH)

    for device in (at_x(x + 1), at_x(x - 1), at_z(z + 1), at_z(z - 1), at_y(y + 1), at_y(y - 1), partner):
        greet(device)
    expected = jnp.int32(7)
    for i in range(8):
        offset = kind + 4 * i
        if i == 0:
            @pl.when(offset != 0)
            def _():
                greet(at_rank(d - offset))
        else:
            greet(at_rank(d - offset))
    expected = expected + jnp.where(kind == 0, 7, 8)
    for e in range(2):
        source_x = 2 * c + e

        @pl.when(jnp.logical_not(diagonal & (source_x == x)))
        def _():
            greet((z * NX + source_x, y * 2 + final_core))
    expected = expected + jnp.where(diagonal, 1, 2)

    @pl.when(z != y)
    def _():
        greet(at_z(y))
    expected = expected + jnp.where(z == y, 7, 0)
    pl.semaphore_wait(barrier, expected)


    def weights():
        send(wt_h, w_v.at[x], at_x(x + 1), W0)
        send(wt_h, w_v.at[x], at_x(x - 1), W0 + 1)
        yield
        half = COLS // 2
        low, high = rem(x + NX - 1, NX), rem(x + 1, NX)
        arrived(w_v.at[low], W0)
        send(w_v.at[low, pl.ds(0, half)], w_v.at[low, pl.ds(0, half)], at_x(x + 1), W0 + 2)
        arrived(w_v.at[high], W0 + 1)
        send(w_v.at[high, pl.ds(half, half)], w_v.at[high, pl.ds(half, half)], at_x(x - 1), W0 + 3)
        yield
        far = rem(x + 2, NX)
        arrived(w_v.at[far, pl.ds(0, half)], W0 + 2)
        arrived(w_v.at[far, pl.ds(half, half)], W0 + 3)
        loads["w"].wait()
        yield

    def ring(block, first, second, me, n, device, base, after=None):
        send(block(me), block(me), device(me + 1), base)
        send(block(me), block(me), device(me - 1), base + 1)
        yield
        for s in (1, 2, 3):
            low, high = rem(me + n - s, n), rem(me + s, n)
            arrived(block(low), base + 2 * s - 2)
            part = block if s < 3 else first
            send(part(low), part(low), device(me + 1), base + 2 * s)
            arrived(block(high), base + 2 * s - 1)
            part = block if s < 3 else second
            send(part(high), part(high), device(me - 1), base + 2 * s + 1)
            if after is not None:
                after(block(low), 2 * s - 2)
                after(block(high), 2 * s - 1)
            yield
        far = rem(me + 4, n)
        arrived(first(far), base + 6)
        arrived(second(far), base + 7)
        if after is not None:
            after(first(far), 6)
            after(second(far), 7)
        yield

    def pages():
        loads["pool"].wait()
        for i in range(8):
            offset = kind + 4 * i
            stage[i] = pool_v[leave_s[offset * 4 + quarter]]

            def go():
                remote(stage.at[i], arr.at[t * 8 + i], at_rank(d + offset), PD + i).start()
            if i == 0:
                pl.when(offset != 0)(go)

                @pl.when(offset == 0)
                def _():
                    arr[t * 8] = jnp.zeros((PAGE, LAT), arr.dtype)
            else:
                go()
        yield
        for i in range(8):
            def come():
                copy = remote(stage.at[i], arr.at[t * 8 + i], partner, PD + i)
                copy.wait_send()
                copy.wait_recv()
            if i == 0:
                pl.when(kind != 0)(come)
            else:
                come()

        def block(o, core=c):
            return arr.at[pl.ds((o * 2 + core) * 8, 8)]

        def first(o, core=c):
            return arr.at[pl.ds((o * 2 + core) * 8, 4)]

        def second(o, core=c):
            return arr.at[pl.ds((o * 2 + core) * 8 + 4, 4)]

        def hand(part, slot):
            send(part, part, partner, PC + 1 + slot)

        send(block(y), block(y), partner, PC)
        yield from ring(block, first, second, y, NY, at_y, PY, hand)
        other = 1 - c
        arrived(block(y, other), PC)
        for s in (1, 2, 3):
            arrived(block(rem(y + NY - s, NY), other), PC + 2 * s - 1)
            arrived(block(rem(y + s, NY), other), PC + 2 * s)
        far = rem(y + 4, NY)
        arrived(first(far, other), PC + 7)
        arrived(second(far, other), PC + 8)
        copy = pltpu.make_async_copy(arr, arr_o, lsem.at[7])
        copy.start()
        loads["arr"] = copy
        yield

    def prefix_part(n):
        def place(j, _):
            slot = perm_s[n * CH + j]
            q_f[j] = q_v[slot].astype(jnp.float32)
            prefix = prefix_s[slot]
            rowinfo[0, j] = jnp.full((HEADS, 128), prefix, jnp.int32)
            rowinfo[1, j] = jnp.full((HEADS, 128), limit_s[prefix], jnp.int32)
            rowinfo[2, j] = jnp.full((HEADS, 128), length_s[slot], jnp.int32)
            return 0

        lax.fori_loop(0, CH, place, 0)
        q = q_f[...].reshape(ROWS, LAT).astype(jnp.bfloat16)
        which = rowinfo[0].reshape(ROWS, 128)[:, :1] == 0
        limit = rowinfo[1].reshape(ROWS, 128)[:, :1]
        scores = jnp.where(
            which,
            jnp.dot(q, kt_v[0], preferred_element_type=jnp.float32),
            jnp.dot(q, kt_v[1], preferred_element_type=jnp.float32),
        ) * SCALE
        column = lax.broadcasted_iota(jnp.int32, (ROWS, PLEN), 1)
        scores = jnp.where(column < limit, scores, MASKED)
        highest = jnp.max(scores, axis=1, keepdims=True)
        raised = jnp.exp(scores - highest)
        total = jnp.sum(raised, axis=1, keepdims=True)
        stats[0] = jnp.broadcast_to(highest, (ROWS, 128))
        stats[1] = jnp.broadcast_to(total, (ROWS, 128))
        blend[...] = lax.dot_general(
            jnp.where(which, raised, 0.0).astype(jnp.bfloat16), kt_v[0, :KVL, :], NT,
            preferred_element_type=jnp.float32,
        ) + lax.dot_general(
            jnp.where(which, 0.0, raised).astype(jnp.bfloat16), kt_v[1, :KVL, :], NT,
            preferred_element_type=jnp.float32,
        )

    def own_part(n):
        def place(j, _):
            at = pl.multiple_of(j * 2 * PAGE, 2 * PAGE)
            if n < CHUNKS - 1:
                slot = perm_s[n * CH + j]
                keys[pl.ds(at, PAGE), :] = pool_v[page_s[slot]]
                keys[pl.ds(at + PAGE, PAGE), :] = pool_v[page_s[REQ + slot]]
            else:
                keys[pl.ds(at, PAGE), :] = arr[arrive_s[2 * j]]
                keys[pl.ds(at + PAGE, PAGE), :] = arr[arrive_s[2 * j + 1]]
            return 0

        lax.fori_loop(0, CH, place, 0)
        group = 64
        row = lax.broadcasted_iota(jnp.int32, (group, 256), 0)
        column = lax.broadcasted_iota(jnp.int32, (group, 256), 1)
        same = lax.shift_right_logical(row, 3) == lax.shift_right_logical(column, 5)
        token = column & 31
        for g in range(ROWS // group):
            rows = pl.ds(g * group, group)
            q = q_f[pl.ds(g * 8, 8)].reshape(group, LAT).astype(jnp.bfloat16)
            k = keys[pl.ds(g * 256, 256), :]
            length = rowinfo[2, pl.ds(g * 8, 8)].reshape(group, 128)[:, :1]
            scores = lax.dot_general(q, k, NT, preferred_element_type=jnp.float32) * SCALE
            scores = jnp.where(same & (token < length), scores, MASKED)
            high_own = jnp.max(scores, axis=1, keepdims=True)
            raised = jnp.exp(scores - high_own)
            total_own = jnp.sum(raised, axis=1, keepdims=True)
            blend_own = jnp.dot(
                raised.astype(jnp.bfloat16), keys[pl.ds(g * 256, 256), :KVL], preferred_element_type=jnp.float32
            )
            high_pre = stats[0, rows, :][:, :1]
            total_pre = stats[1, rows, :][:, :1]
            ceiling = jnp.maximum(high_pre, high_own)
            f = jnp.exp(high_pre - ceiling)
            h = jnp.exp(high_own - ceiling)
            mixed = (f * blend[rows, :] + h * blend_own) / (f * total_pre + h * total_own)
            for l in range(KVL // 128):
                merged[l, rows, :] = mixed[:, l * 128:(l + 1) * 128]
        mine = pl.ds(pl.multiple_of(z * CH, CH), CH)
        for h in range(HEADS):
            a = jnp.concatenate(
                [merged[l, pl.ds(h, CH, stride=HEADS), :] for l in range(KVL // 128)], axis=1
            ).astype(jnp.bfloat16)
            zb[n, mine, h * VH:(h + 1) * VH] = jnp.dot(
                a, vup_v[h], preferred_element_type=jnp.float32
            ).astype(jnp.bfloat16)

    def heads(n):
        def block(o):
            return zb.at[n, pl.ds(pl.multiple_of(o * CH, CH), CH)]

        def first(o):
            return zb.at[n, pl.ds(pl.multiple_of(o * CH, CH), CH // 2)]

        def second(o):
            return zb.at[n, pl.ds(pl.multiple_of(o * CH + CH // 2, CH // 2), CH // 2)]

        yield from ring(block, first, second, z, NZ, at_z, Z0 + 8 * n)

    def product(n):
        for i in range(2):
            sx[n, i] = lax.dot_general(
                zb[n], w_v[2 * (1 - c) + i], NT, preferred_element_type=jnp.float32
            ).astype(jnp.bfloat16)
        send(sx.at[n], rx.at[n], partner, CX + n)
        for i in range(2):
            own[n, i] = lax.dot_general(zb[n], w_v[2 * c + i], NT, preferred_element_type=jnp.float32)

    def sums(n):
        base = RS + 8 * n
        arrived(rx.at[n], CX + n)
        for i in range(2):
            own[n, i] = own[n, i] + rx[n, i].astype(jnp.float32)

        def mine(i, o):
            return own[n, i, pl.ds(pl.multiple_of(rem(o + 2 * NY, NY) * CH, CH), CH), :]

        up, down = at_y(y + 1), at_y(y - 1)
        ss[n, 0, 0, 0] = mine(0, y + 4).astype(jnp.bfloat16)
        send(ss.at[n, 0, 0, 0], rr.at[n, 0, 0, 0], up, base)
        ss[n, 1, 0, 1] = mine(1, y - 4).astype(jnp.bfloat16)
        send(ss.at[n, 1, 0, 1], rr.at[n, 1, 0, 1], down, base + 1)
        yield
        arrived(rr.at[n, 0, 0, 0], base)
        ss[n, 0, 1, 0] = (mine(0, y + 3) + rr[n, 0, 0, 0].astype(jnp.float32)).astype(jnp.bfloat16)
        ss[n, 0, 1, 1] = mine(1, y + 3).astype(jnp.bfloat16)
        send(ss.at[n, 0, 1], rr.at[n, 0, 1], up, base + 2)
        arrived(rr.at[n, 1, 0, 1], base + 1)
        ss[n, 1, 1, 1] = (mine(1, y - 3) + rr[n, 1, 0, 1].astype(jnp.float32)).astype(jnp.bfloat16)
        ss[n, 1, 1, 0] = mine(0, y - 3).astype(jnp.bfloat16)
        send(ss.at[n, 1, 1], rr.at[n, 1, 1], down, base + 3)
        yield
        for s in (2, 3):
            for way, device, o in ((0, up, y + 4 - s), (1, down, y - 4 + s)):
                arrived(rr.at[n, way, s - 1], base + 2 * (s - 1) + way)
                for i in range(2):
                    ss[n, way, s, i] = (mine(i, o) + rr[n, way, s - 1, i].astype(jnp.float32)).astype(jnp.bfloat16)
                send(ss.at[n, way, s], rr.at[n, way, s], device, base + 2 * s + way)
            yield
        arrived(rr.at[n, 0, 3], base + 6)
        arrived(rr.at[n, 1, 3], base + 7)
        for i in range(2):
            red[i, n * CH:(n + 1) * CH] = (
                mine(i, y) + rr[n, 0, 3, i].astype(jnp.float32) + rr[n, 1, 3, i].astype(jnp.float32)
            ).astype(jnp.bfloat16)
        yield

    def order_send():
        loads["order"].wait()

        @pl.when(z == y)
        def _():
            for s in range(1, NZ):
                remote(order_v, order_r, at_z(z + s), PM + s - 1, PM).start()

    def order_wait():
        @pl.when(z == y)
        def _():
            for s in range(1, NZ):
                remote(order_v, order_r, at_z(z + s), PM + s - 1, PM).wait_send()
            order_r[...] = order_v[...]

        @pl.when(z != y)
        def _():
            remote(order_v, order_r, at_z(y), PM, PM).wait_recv()

    def finish():
        order_wait()
        place = order_r[...][:, :REQ]
        slot = rem(x, 2)
        for i in range(2):
            fx[i] = jnp.dot(place, red[i], preferred_element_type=jnp.float32).astype(jnp.bfloat16)
            same = diagonal & (2 * c + i == x)
            copy = remote(fx.at[i], fr.at[slot], (z * NX + 2 * c + i, y * 2 + final_core), FX + i, FX + slot)

            @pl.when(same)
            def _():
                fr[slot] = fx[i]

            pl.when(jnp.logical_not(same))(copy.start)
        loads["res"].wait()
        for e in range(2):
            same = diagonal & (2 * c + e == x)
            copy = remote(fx.at[e], fr.at[e], partner, FX + e)
            pl.when(jnp.logical_not(same))(copy.wait_recv)
            rows = pl.ds(e * REQ, REQ)
            out_ref[rows, :] = (
                res_v[rows, :].astype(jnp.float32) + fr[e].astype(jnp.float32)
            ).astype(jnp.bfloat16)
        for i in range(2):
            same = diagonal & (2 * c + i == x)
            copy = remote(fx.at[i], fr.at[slot], partner, FX + i)
            pl.when(jnp.logical_not(same))(copy.wait_send)

    w = weights()
    p = pages()
    hs = [heads(n) for n in range(CHUNKS)]
    rs = [sums(n) for n in range(CHUNKS)]

    next(w)
    next(p)
    order_send()
    loads["q"].wait()
    loads["kt"].wait()
    prefix_part(0)
    loads["vup"].wait()
    own_part(0)
    next(hs[0])
    next(p)
    prefix_part(1)
    own_part(1)
    next(hs[1])
    next(p)
    next(w)
    next(hs[0])
    prefix_part(2)
    next(p)
    next(hs[0])
    next(hs[1])
    next(p)
    next(hs[0])
    next(hs[1])
    next(w)
    next(p)
    next(p)
    own_part(2)
    next(hs[2])
    next(hs[0])
    next(hs[1])
    product(0)
    next(hs[2])
    next(hs[1])
    next(rs[0])
    product(1)
    next(hs[2])
    next(rs[0])
    next(rs[1])
    next(hs[2])
    next(rs[0])
    next(rs[1])
    next(hs[2])
    product(2)
    next(rs[0])
    next(rs[1])
    next(rs[2])
    next(rs[0])
    next(rs[1])
    next(rs[2])
    next(rs[1])
    next(rs[2])
    next(rs[2])
    next(rs[2])
    finish()
    for copy in sent:
        copy.wait_send()
    loads["arr"].wait()


def place_pages(page_s, move_s, pool_h, arr_h, new_h, pool_v, sem):
    rank = lax.axis_index("dp")
    load = pltpu.make_async_copy(pool_h, pool_v, sem.at[0])
    load.start()
    load.wait()

    def come(k, _):
        slot = move_s[k]
        offset = rem(move_s[MOVES + k] - rank + 32, 32)
        source = (rem(offset, 4) * 4 + 2 * rem(k, 2)) * 8 + div(offset, 4)
        for p in range(2):
            pltpu.make_async_copy(arr_h.at[source + 8 * p], pool_v.at[page_s[p * REQ + slot]], sem.at[1]).start()
        return 0

    lax.fori_loop(0, MOVES, come, 0)
    pltpu.make_async_copy(arr_h.at[pl.ds(0, 2 * MOVES)], pool_v.at[pl.ds(0, 2 * MOVES)], sem.at[1]).wait()
    store = pltpu.make_async_copy(pool_v, new_h, sem.at[2])
    store.start()
    store.wait()


def local(
    queries, page_pool, prefix_cache, page_table, lengths, prefix_id, prefix_len,
    move_list, value_up, output_weight, residual,
):
    rank = lax.axis_index("dp")
    leaving = move_list[0, :, 0]
    offset = (move_list[0, :, 1] - rank + 32) % 32
    slots = jnp.arange(REQ, dtype=jnp.int32)
    moves = jnp.arange(MOVES, dtype=jnp.int32)
    is_left = leaving[None, :] == slots[:, None]
    left = jnp.any(is_left, axis=1)
    move_of = jnp.sum(jnp.where(is_left, moves[None, :], 0), axis=1)
    ahead = jnp.sum(jnp.where((slots[None, :] < slots[:, None]) & ~left[None, :], 1, 0), axis=1)
    position = jnp.where(left, REQ - MOVES + move_of, ahead)
    perm = jnp.sum(jnp.where(position[None, :] == slots[:, None], slots[None, :], 0), axis=1)
    order = (position[:, None] == jnp.arange(128, dtype=jnp.int32)[None, :]).astype(jnp.bfloat16)
    pages = page_table.T
    left_pages = jnp.sum(jnp.where(is_left[None, :, :], pages[:, :, None], 0), axis=1)
    by_pair = left_pages.reshape(2, 16, 2)
    hit = offset[::2][None, :] == jnp.arange(32, dtype=jnp.int32)[:, None]
    leave = jnp.sum(jnp.where(hit[:, :, None, None], by_pair.transpose(1, 2, 0)[None], 0), axis=1)
    arrive = ((offset % 4) * 4 + 2 * (moves % 2))[:, None] + jnp.arange(2, dtype=jnp.int32)[None, :]
    arrive = arrive * 8 + (offset // 4)[:, None]
    pages = pages.reshape(-1)
    arrive = arrive.reshape(-1)

    smem = pl.BlockSpec(memory_space=pltpu.SMEM)
    hbm = pl.BlockSpec(memory_space=pl.ANY)
    bf, f32 = jnp.bfloat16, jnp.float32
    vm = pltpu.VMEM
    layer_out, arr = pl.pallas_call(
        fused,
        out_shape=(
            jax.ShapeDtypeStruct((2 * REQ, COLS), bf),
            jax.ShapeDtypeStruct((128, PAGE, LAT), bf),
        ),
        in_specs=[smem] * 7 + [hbm] * 7,
        out_specs=(pl.BlockSpec(memory_space=pltpu.VMEM), hbm),
        scratch_shapes=[
            vm((REQ, HEADS, LAT), bf), vm((POOL, PAGE, LAT), bf), vm((2, LAT, PLEN), bf),
            vm((HEADS, KVL, VH), bf), vm((NX, COLS, DEPTH), bf), vm((REQ, 128), bf),
            vm((2 * REQ, COLS), bf), vm((REQ, 128), bf),
            vm((8, PAGE, LAT), bf), vm((128, PAGE, LAT), bf), vm((CH, HEADS, LAT), f32),
            vm((CH * 2 * PAGE, LAT), bf), vm((3, CH, HEADS, 128), jnp.int32), vm((ROWS, KVL), f32),
            vm((2, ROWS, 128), f32), vm((KVL // 128, ROWS, 128), f32),
            vm((CHUNKS, NZ * CH, DEPTH), bf), vm((CHUNKS, 2, NZ * CH, COLS), bf),
            vm((CHUNKS, 2, NZ * CH, COLS), bf), vm((CHUNKS, 2, NZ * CH, COLS), f32),
            vm((CHUNKS, 2, 4, 2, CH, COLS), bf), vm((CHUNKS, 2, 4, 2, CH, COLS), bf),
            vm((2, REQ, COLS), bf), vm((2, REQ, COLS), bf), vm((2, REQ, COLS), bf),
            pltpu.SemaphoreType.DMA((8,)),
            pltpu.SemaphoreType.DMA((SEMS,)),
            pltpu.SemaphoreType.DMA((SEMS,)),
        ],
        compiler_params=pltpu.CompilerParams(
            collective_id=0, has_side_effects=True, vmem_limit_bytes=60 * 1024 * 1024
        ),
        name="attention_block",
    )(
        perm, pages, prefix_id, lengths, prefix_len, leave.reshape(-1), arrive,
        queries, page_pool, prefix_cache.transpose(0, 2, 1), value_up, output_weight.T, order, residual,
    )
    new_pool = pl.pallas_call(
        place_pages,
        out_shape=jax.ShapeDtypeStruct((POOL, PAGE, LAT), bf),
        in_specs=[smem] * 2 + [hbm] * 2,
        out_specs=hbm,
        scratch_shapes=[vm((POOL, PAGE, LAT), bf), pltpu.SemaphoreType.DMA((3,))],
        compiler_params=pltpu.CompilerParams(vmem_limit_bytes=60 * 1024 * 1024),
        name="place_pages",
    )(pages, move_list[0].T.reshape(-1), page_pool, arr)
    return (layer_out, new_pool)


def solution(mesh):
    in_specs = (
        P("dp", "tp", None),
        P("dp", None, None),
        P(),
        P("dp", None),
        P("dp"),
        P("dp"),
        P(),
        P("dp", None, None),
        P("tp", None, None),
        P("tp", "dp"),
        P("tp", "dp"),
    )
    out_specs = (P("tp", "dp"), P("dp", None, None))
    return jax.shard_map(local, mesh=mesh, in_specs=in_specs, out_specs=out_specs, check_vma=False)
```

```python
import functools

import jax
import jax.numpy as jnp
from jax import lax
from jax.experimental import pallas as pl
from jax.experimental.pallas import tpu as pltpu
from jax.sharding import PartitionSpec as P

MESH = pl.DeviceIdType.MESH

LAT = 576
KVL = 512
HEADS = 8
VH = 128
PAGE = 16
REQ = 96
MOVES = 32
CH = 32
CHUNKS = REQ // CH
ROWS = CH * HEADS
POOL = 192
PLEN = 384
NZ, NX, NY = 8, 4, 8
COLS = 224
DEPTH = HEADS * VH
SCALE = 192.0 ** (-0.5)
MASKED = -1e30

NT = (((1,), (1,)), ((), ()))

W0 = 0
PD = W0 + 4
PY = PD + 8
PC = PY + 14
Z0 = PC + 15
CX = Z0 + 8 * CHUNKS
RS = CX + CHUNKS
OR = RS + 16 * CHUNKS
SEMS = OR + 16


def div(a, n):
    return lax.div(a, jnp.int32(n))


def rem(a, n):
    return lax.rem(a, jnp.int32(n))


def fused(
    page_s, prefix_s, length_s, limit_s,
    page_r, move_r,
    q_h, pool_h, kt_h, vup_h, wt_h, res_h,
    out_ref, come_o,
    q_v, pool_v, kt_v, vup_v, w_v, res_v, order_v, order_r,
    table_v, table_s,
    stage, arr, q_f, keys, rowinfo, blend, stats, merged,
    zb, sx, rx, own, ss, rr, red,
    lsem, ssem, rsem,
):
    d = lax.axis_index("dp")
    t = lax.axis_index("tp")
    z, x = div(d, NX), rem(d, NX)
    y, c = div(t, 2), rem(t, 2)
    kind, quarter = div(t, 4), rem(t, 4)

    def at_x(v):
        return (z * NX + rem(v + NX, NX), t)

    def at_z(v):
        return (rem(v + NZ, NZ) * NX + x, t)

    def at_y(v):
        return (d, rem(v + NY, NY) * 2 + c)

    def at_rank(v):
        return (rem(v + 32, 32), t)

    partner = (d, y * 2 + 1 - c)
    final_core = div(x, 2)
    diagonal = c == final_core

    sent = []

    def remote(src, dst, device, slot, recv_slot=None):
        return pltpu.make_async_remote_copy(
            src_ref=src, dst_ref=dst, send_sem=ssem.at[slot],
            recv_sem=rsem.at[slot if recv_slot is None else recv_slot],
            device_id=device, device_id_type=MESH,
        )

    def send(src, dst, device, slot):
        copy = remote(src, dst, device, slot)
        copy.start()
        sent.append(copy)

    def arrived(dst, slot):
        remote(dst, dst, partner, slot).wait_recv()

    def owner(core, e, s):
        return (z * NX + 2 * core + e, rem(y + s + NY, NY) * 2 + final_core)

    def itself(e):
        return diagonal & (2 * c + e == x)

    def order_itself(e):
        return (z == y) & (2 * c + e == x) & (rem(z, 2) == c)

    barrier = pltpu.get_barrier_semaphore()

    def greet(device):
        pl.semaphore_signal(barrier, inc=1, device_id=device, device_id_type=MESH)

    for i in range(8):
        offset = kind + 4 * i
        if i == 0:
            @pl.when(offset != 0)
            def _():
                greet(at_rank(d - offset))
        else:
            greet(at_rank(d - offset))
    for device in (
        at_x(x + 1), at_x(x - 1), at_z(z + 1), at_z(z - 1), at_z(z + 2), at_z(z - 2),
        at_y(y + 1), at_y(y - 1), partner,
    ):
        greet(device)
    for s in range(NY):
        for e in range(2):
            source = (z * NX + 2 * c + e, rem(y - s + NY, NY) * 2 + final_core)
            if s == 0:
                @pl.when(jnp.logical_not(itself(e)))
                def _():
                    greet(source)
            else:
                greet(source)
    for e in range(2):
        @pl.when(jnp.logical_not(order_itself(e)))
        def _():
            greet((y * NX + 2 * c + e, y * 2 + rem(z, 2)))

    loads = {}
    for n, (name, src, dst) in enumerate([
        ("pool", pool_h, pool_v), ("q", q_h, q_v), ("kt", kt_h, kt_v), ("vup", vup_h, vup_v),
        ("w", wt_h, w_v.at[x]), ("res", res_h, res_v),
    ]):
        loads[name] = pltpu.make_async_copy(src, dst, lsem.at[n])
        loads[name].start()

    def iota(shape, dim):
        return lax.broadcasted_iota(jnp.int32, shape, dim)

    def column_of(row, n):
        return jnp.sum(jnp.where(iota((n, n), 0) == iota((n, n), 1), row, 0), axis=1, keepdims=True)

    leaving = move_r[0]
    ahead_by = move_r[1] - d
    offsets = jnp.where(ahead_by < 0, ahead_by + 32, ahead_by)
    leaving_column = column_of(leaving, MOVES)
    offset_column = column_of(offsets, MOVES)
    is_left = iota((REQ, MOVES), 0) == leaving
    left = jnp.sum(jnp.where(is_left, 1, 0), axis=1, keepdims=True)
    move_of = jnp.sum(jnp.where(is_left, iota((REQ, MOVES), 1), 0), axis=1, keepdims=True)
    by_move = iota((MOVES, REQ), 1) == leaving_column
    left_row = jnp.sum(jnp.where(by_move, 1, 0), axis=0, keepdims=True)
    before = jnp.sum(
        jnp.where(iota((REQ, REQ), 1) < iota((REQ, REQ), 0), 1 - left_row, 0), axis=1, keepdims=True
    )
    position = jnp.where(left > 0, REQ - MOVES + move_of, before)
    placed = position == iota((REQ, 128), 1)
    order_v[...] = jnp.where(placed, 1.0, 0.0).astype(jnp.bfloat16)
    perm = jnp.sum(jnp.where(placed, iota((REQ, 128), 0), 0), axis=0, keepdims=True)
    table_v[0:1, :] = perm
    parity = lax.broadcasted_iota(jnp.int32, (MOVES, MOVES), 0) & 1
    for p in range(2):
        row = page_r[p:p + 1, :]
        moved_page = jnp.sum(jnp.where(by_move, row, 0), axis=1, keepdims=True)
        for b in range(2):
            hit = (offset_column == iota((MOVES, MOVES), 1)) & (parity == b)
            table_v[1 + 2 * b + p:2 + 2 * b + p, :MOVES] = jnp.sum(
                jnp.where(hit, moved_page, 0), axis=0, keepdims=True
            )
        b = lax.broadcasted_iota(jnp.int32, (1, MOVES), 1) & 1
        table_v[5 + p:6 + p, :MOVES] = (
            ((offsets & 3) * 4 + 2 * b + p) * 8 + lax.shift_right_logical(offsets, 2)
        )
    to_scalar = pltpu.make_async_copy(table_v, table_s, lsem.at[6])
    to_scalar.start()

    expected = 9 + jnp.where(kind == 0, 7, 8) + jnp.where(diagonal, 15, 16)
    expected = expected + jnp.where(z == y, jnp.where(diagonal & (rem(z, 2) == c), 15, 16), 0)
    pl.semaphore_wait(barrier, expected)
    to_scalar.wait()

    def listed(row, at, size):
        return jnp.clip(table_s[row, at], 0, size - 1)


    def weights():
        send(wt_h, w_v.at[x], at_x(x + 1), W0)
        send(wt_h, w_v.at[x], at_x(x - 1), W0 + 1)
        yield
        half = COLS // 2
        low, high = rem(x + NX - 1, NX), rem(x + 1, NX)
        arrived(w_v.at[low], W0)
        send(w_v.at[low, pl.ds(0, half)], w_v.at[low, pl.ds(0, half)], at_x(x + 1), W0 + 2)
        arrived(w_v.at[high], W0 + 1)
        send(w_v.at[high, pl.ds(half, half)], w_v.at[high, pl.ds(half, half)], at_x(x - 1), W0 + 3)
        yield
        far = rem(x + 2, NX)
        arrived(w_v.at[far, pl.ds(0, half)], W0 + 2)
        arrived(w_v.at[far, pl.ds(half, half)], W0 + 3)
        loads["w"].wait()
        yield

    def pages_out():
        loads["pool"].wait()
        for i in range(8):
            offset = kind + 4 * i
            stage[i] = pool_v[listed(1 + quarter, offset, POOL)]

            def go():
                remote(stage.at[i], arr.at[t * 8 + i], at_rank(d + offset), PD + i).start()
            if i == 0:
                pl.when(offset != 0)(go)

                @pl.when(offset == 0)
                def _():
                    arr[t * 8] = jnp.zeros((PAGE, LAT), arr.dtype)
            else:
                go()
        yield
        for i in range(8):
            def come():
                copy = remote(stage.at[i], arr.at[t * 8 + i], partner, PD + i)
                copy.wait_send()
                copy.wait_recv()
            if i == 0:
                pl.when(kind != 0)(come)
            else:
                come()

    def pages_ring():
        def part(o, half, core=c):
            return arr.at[pl.ds((o * 2 + core) * 8 + 4 * half, 4)]

        def block(o, core=c):
            return arr.at[pl.ds((o * 2 + core) * 8, 8)]

        devices = (at_y(y + 1), at_y(y - 1))
        for half in range(2):
            for way in range(2):
                send(part(y, half), part(y, half), devices[way], PY + 2 * half + way)
        send(block(y), block(y), partner, PC)
        yield
        for s in (1, 2, 3):
            for half in range(2):
                for way, o in ((0, rem(y + NY - s, NY)), (1, rem(y + s, NY))):
                    slot = 4 * (s - 1) + 2 * half + way
                    arrived(part(o, half), PY + slot)
                    if s < 3:
                        send(part(o, half), part(o, half), devices[way], PY + slot + 4)
                    elif half == way:
                        send(part(o, half), part(o, half), devices[way], PY + 12 + way)
                    send(part(o, half), part(o, half), partner, PC + 1 + slot)
                yield
        far = rem(y + 4, NY)
        for half in range(2):
            arrived(part(far, half), PY + 12 + half)
            send(part(far, half), part(far, half), partner, PC + 13 + half)
        other = 1 - c
        arrived(block(y, other), PC)
        for s in (1, 2, 3):
            for half in range(2):
                for way, o in ((0, rem(y + NY - s, NY)), (1, rem(y + s, NY))):
                    arrived(part(o, half, other), PC + 1 + 4 * (s - 1) + 2 * half + way)
        for half in range(2):
            arrived(part(far, half, other), PC + 13 + half)
        yield

    def prefix_part(n):
        def place(j, _):
            slot = listed(0, n * CH + j, REQ)
            q_f[j] = q_v[slot].astype(jnp.float32)
            prefix = prefix_s[slot]
            rowinfo[0, j] = jnp.full((HEADS, 128), prefix, jnp.int32)
            rowinfo[1, j] = jnp.full((HEADS, 128), limit_s[prefix], jnp.int32)
            rowinfo[2, j] = jnp.full((HEADS, 128), length_s[slot], jnp.int32)
            return 0

        lax.fori_loop(0, CH, place, 0)
        q = q_f[...].reshape(ROWS, LAT).astype(jnp.bfloat16)
        which = rowinfo[0].reshape(ROWS, 128)[:, :1] == 0
        limit = rowinfo[1].reshape(ROWS, 128)[:, :1]
        scores = jnp.where(
            which,
            jnp.dot(q, kt_v[0], preferred_element_type=jnp.float32),
            jnp.dot(q, kt_v[1], preferred_element_type=jnp.float32),
        ) * SCALE
        column = lax.broadcasted_iota(jnp.int32, (ROWS, PLEN), 1)
        scores = jnp.where(column < limit, scores, MASKED)
        highest = jnp.max(scores, axis=1, keepdims=True)
        raised = jnp.exp(scores - highest)
        total = jnp.sum(raised, axis=1, keepdims=True)
        stats[0] = jnp.broadcast_to(highest, (ROWS, 128))
        stats[1] = jnp.broadcast_to(total, (ROWS, 128))
        blend[...] = lax.dot_general(
            jnp.where(which, raised, 0.0).astype(jnp.bfloat16), kt_v[0, :KVL, :], NT,
            preferred_element_type=jnp.float32,
        ) + lax.dot_general(
            jnp.where(which, 0.0, raised).astype(jnp.bfloat16), kt_v[1, :KVL, :], NT,
            preferred_element_type=jnp.float32,
        )

    def own_part(n):
        def place(j, _):
            at = pl.multiple_of(j * 2 * PAGE, 2 * PAGE)
            if n < CHUNKS - 1:
                slot = listed(0, n * CH + j, REQ)
                keys[pl.ds(at, PAGE), :] = pool_v[page_s[0, slot]]
                keys[pl.ds(at + PAGE, PAGE), :] = pool_v[page_s[1, slot]]
            else:
                keys[pl.ds(at, PAGE), :] = arr[listed(5, j, 128)]
                keys[pl.ds(at + PAGE, PAGE), :] = arr[listed(6, j, 128)]
            return 0

        lax.fori_loop(0, CH, place, 0)
        if n == CHUNKS - 1:
            loads["come"] = pltpu.make_async_copy(keys, come_o, lsem.at[7])
            loads["come"].start()
        group = 64
        row = lax.broadcasted_iota(jnp.int32, (group, 256), 0)
        column = lax.broadcasted_iota(jnp.int32, (group, 256), 1)
        same = lax.shift_right_logical(row, 3) == lax.shift_right_logical(column, 5)
        token = column & 31
        for g in range(ROWS // group):
            rows = pl.ds(g * group, group)
            q = q_f[pl.ds(g * 8, 8)].reshape(group, LAT).astype(jnp.bfloat16)
            k = keys[pl.ds(g * 256, 256), :]
            length = rowinfo[2, pl.ds(g * 8, 8)].reshape(group, 128)[:, :1]
            scores = lax.dot_general(q, k, NT, preferred_element_type=jnp.float32) * SCALE
            scores = jnp.where(same & (token < length), scores, MASKED)
            high_own = jnp.max(scores, axis=1, keepdims=True)
            raised = jnp.exp(scores - high_own)
            total_own = jnp.sum(raised, axis=1, keepdims=True)
            blend_own = jnp.dot(
                raised.astype(jnp.bfloat16), keys[pl.ds(g * 256, 256), :KVL], preferred_element_type=jnp.float32
            )
            high_pre = stats[0, rows, :][:, :1]
            total_pre = stats[1, rows, :][:, :1]
            ceiling = jnp.maximum(high_pre, high_own)
            f = jnp.exp(high_pre - ceiling)
            h = jnp.exp(high_own - ceiling)
            mixed = (f * blend[rows, :] + h * blend_own) / (f * total_pre + h * total_own)
            for l in range(KVL // 128):
                merged[l, rows, :] = mixed[:, l * 128:(l + 1) * 128]
        mine = pl.ds(pl.multiple_of(z * CH, CH), CH)
        for h in range(HEADS):
            a = jnp.concatenate(
                [merged[l, pl.ds(h, CH, stride=HEADS), :] for l in range(KVL // 128)], axis=1
            ).astype(jnp.bfloat16)
            zb[n, mine, h * VH:(h + 1) * VH] = jnp.dot(
                a, vup_v[h], preferred_element_type=jnp.float32
            ).astype(jnp.bfloat16)

    def heads(n):
        def block(o):
            return zb.at[n, pl.ds(pl.multiple_of(o * CH, CH), CH)]

        def half(o, i):
            return zb.at[n, pl.ds(pl.multiple_of(o * CH + i * (CH // 2), CH // 2), CH // 2)]

        base = Z0 + 8 * n
        low = [rem(z + NZ - s, NZ) for s in range(4)]
        high = [rem(z + s, NZ) for s in range(5)]
        for s in (2, 1):
            send(block(z), block(z), at_z(z + s), base + 2 * s - 2)
            send(block(z), block(z), at_z(z - s), base + 2 * s - 1)
        yield
        arrived(block(low[2]), base + 2)
        send(block(low[2]), block(low[2]), at_z(z + 1), base + 4)
        send(half(low[2], 0), half(low[2], 0), at_z(z + 2), base + 6)
        arrived(block(high[2]), base + 3)
        send(block(high[2]), block(high[2]), at_z(z - 1), base + 5)
        send(half(high[2], 1), half(high[2], 1), at_z(z - 2), base + 7)
        yield
        arrived(block(low[1]), base)
        arrived(block(high[1]), base + 1)
        arrived(block(low[3]), base + 4)
        arrived(block(high[3]), base + 5)
        arrived(half(high[4], 0), base + 6)
        arrived(half(high[4], 1), base + 7)
        yield

    def product(n):
        for i in range(2):
            sx[n, i] = lax.dot_general(
                zb[n], w_v[2 * (1 - c) + i], NT, preferred_element_type=jnp.float32
            ).astype(jnp.bfloat16)
        send(sx.at[n], rx.at[n], partner, CX + n)
        for i in range(2):
            own[n, i] = lax.dot_general(zb[n], w_v[2 * c + i], NT, preferred_element_type=jnp.float32)

    def sums(n):
        base = RS + 16 * n
        arrived(rx.at[n], CX + n)
        for i in range(2):
            ss[n, i] = (own[n, i] + rx[n, i].astype(jnp.float32)).astype(jnp.bfloat16)
        mine = rem(x, 2)
        for s in (4, 3, 5, 2, 6, 1, 7, 0):
            rows = pl.ds(pl.multiple_of(rem(y + s, NY) * CH, CH), CH)
            for i in range(2):
                copy = remote(
                    ss.at[n, i, rows], rr.at[n, s, mine], owner(c, i, s), base + 2 * s + i, base + 2 * s + mine
                )
                if s == 0:
                    pl.when(jnp.logical_not(itself(i)))(copy.start)

                    @pl.when(itself(i))
                    def _():
                        rr[n, 0, mine] = ss[n, i, rows, :]
                else:
                    copy.start()
                    sent.append(copy)
        yield
        for e in range(2):
            total = None
            for s in (0, 1, 7, 2, 6, 3, 5, 4):
                copy = remote(rr.at[n, s, e], rr.at[n, s, e], partner, base + 2 * s + e)
                if s == 0:
                    pl.when(jnp.logical_not(itself(e)))(copy.wait_recv)
                else:
                    copy.wait_recv()
                part = rr[n, s, e].astype(jnp.float32)
                total = part if total is None else total + part
            red[e, n * CH:(n + 1) * CH] = total
        rows = pl.ds(0, CH)
        for i in range(2):
            copy = remote(ss.at[n, i, rows], ss.at[n, i, rows], partner, base + i)
            pl.when(jnp.logical_not(itself(i)))(copy.wait_send)
        yield

    def order_copies(act):
        mine = rem(x, 2)
        for a in range(4):
            for column in range(NX):
                to = (2 * a + c) * NX + column
                copy = remote(
                    order_v, order_r.at[mine], (to, y * 2 + final_core), OR + 4 * a + column, OR + mine
                )
                pl.when((z == y) & jnp.logical_not(diagonal & (to == d)))(functools.partial(act, copy))

    def order_send():
        order_copies(lambda copy: copy.start())

        @pl.when((z == y) & diagonal & (rem(z, 2) == c))
        def _():
            order_r[rem(x, 2)] = order_v[...]

    def order_wait():
        order_copies(lambda copy: copy.wait_send())
        for e in range(2):
            copy = remote(order_v, order_r.at[e], partner, OR + e)
            pl.when(jnp.logical_not(order_itself(e)))(copy.wait_recv)

    def finish():
        loads["res"].wait()
        for e in range(2):
            place = order_r[e][:, :REQ]
            rows = pl.ds(e * REQ, REQ)
            total = red[e]
            high = total.astype(jnp.bfloat16)
            low = (total - high.astype(jnp.float32)).astype(jnp.bfloat16)
            placed = jnp.dot(place, high, preferred_element_type=jnp.float32) + jnp.dot(
                place, low, preferred_element_type=jnp.float32
            )
            out_ref[rows, :] = (res_v[rows, :].astype(jnp.float32) + placed).astype(jnp.bfloat16)

    w = weights()
    p = pages_out()
    r = pages_ring()
    hs = [heads(n) for n in range(CHUNKS)]
    rs = [sums(n) for n in range(CHUNKS)]

    next(p)
    next(w)
    order_send()
    loads["q"].wait()
    loads["kt"].wait()
    prefix_part(0)
    loads["vup"].wait()
    own_part(0)
    next(hs[0])
    next(p, None)
    next(r)
    prefix_part(1)
    own_part(1)
    next(hs[1])
    next(r)
    next(r)
    next(hs[0])
    next(w)
    next(r)
    next(r)
    prefix_part(2)
    next(hs[1])
    next(r)
    next(r)
    next(w)
    next(r)
    own_part(2)
    next(hs[2])
    next(hs[0])
    product(0)
    next(rs[0])
    next(hs[2])
    next(hs[1])
    product(1)
    next(rs[1])
    next(rs[0])
    order_wait()
    next(hs[2])
    product(2)
    next(rs[1])
    next(rs[2])
    next(rs[2])
    finish()
    for copy in sent:
        copy.wait_send()
    loads["come"].wait()


PARTS = 4


def place_pages(page_s, move_s, pool_h, come_h, new_h, pool_v, come_v, sem):
    size = POOL // PARTS
    come = pltpu.make_async_copy(come_h, come_v, sem.at[2 * PARTS])
    come.start()
    parts = [pl.ds(n * size, size) for n in range(PARTS)]
    loads = [pltpu.make_async_copy(pool_h.at[part], pool_v.at[part], sem.at[n]) for n, part in enumerate(parts)]
    stores = [pltpu.make_async_copy(pool_v.at[part], new_h.at[part], sem.at[PARTS + n]) for n, part in enumerate(parts)]
    for load in loads:
        load.start()
    come.wait()
    for n in range(PARTS):
        loads[n].wait()

        def place(k, _):
            slot = move_s[0, 0, k]
            for p in range(2):
                page = page_s[p, slot]

                @pl.when((page >= n * size) & (page < (n + 1) * size))
                def _():
                    pool_v[page] = come_v[2 * k + p]
            return 0

        lax.fori_loop(0, MOVES, place, 0)
        stores[n].start()
    for store in stores:
        store.wait()


def local(
    queries, page_pool, prefix_cache, page_table, lengths, prefix_id, prefix_len,
    move_list, value_up, output_weight, residual,
):
    pages = page_table.T
    moves = move_list.transpose(2, 0, 1)
    smem = pl.BlockSpec(memory_space=pltpu.SMEM)
    vmem = pl.BlockSpec(memory_space=pltpu.VMEM)
    hbm = pl.BlockSpec(memory_space=pl.ANY)
    bf, f32 = jnp.bfloat16, jnp.float32
    vm = pltpu.VMEM
    layer_out, come = pl.pallas_call(
        fused,
        out_shape=(
            jax.ShapeDtypeStruct((2 * REQ, COLS), bf),
            jax.ShapeDtypeStruct((CH * 2 * PAGE, LAT), bf),
        ),
        in_specs=[smem] * 4 + [vmem] * 2 + [hbm] * 6,
        out_specs=(vmem, hbm),
        scratch_shapes=[
            vm((REQ, HEADS, LAT), bf), vm((POOL, PAGE, LAT), bf), vm((2, LAT, PLEN), bf),
            vm((HEADS, KVL, VH), bf), vm((NX, COLS, DEPTH), bf), vm((2 * REQ, COLS), bf),
            vm((REQ, 128), bf), vm((2, REQ, 128), bf),
            vm((8, 128), jnp.int32), pltpu.SMEM((8, 128), jnp.int32),
            vm((8, PAGE, LAT), bf), vm((128, PAGE, LAT), bf), vm((CH, HEADS, LAT), f32),
            vm((CH * 2 * PAGE, LAT), bf), vm((3, CH, HEADS, 128), jnp.int32), vm((ROWS, KVL), f32),
            vm((2, ROWS, 128), f32), vm((KVL // 128, ROWS, 128), f32),
            vm((CHUNKS, NZ * CH, DEPTH), bf), vm((CHUNKS, 2, NZ * CH, COLS), bf),
            vm((CHUNKS, 2, NZ * CH, COLS), bf), vm((CHUNKS, 2, NZ * CH, COLS), f32),
            vm((CHUNKS, 2, NZ * CH, COLS), bf), vm((CHUNKS, NY, 2, CH, COLS), bf),
            vm((2, REQ, COLS), f32),
            pltpu.SemaphoreType.DMA((8,)),
            pltpu.SemaphoreType.DMA((SEMS,)),
            pltpu.SemaphoreType.DMA((SEMS,)),
        ],
        compiler_params=pltpu.CompilerParams(
            collective_id=0, has_side_effects=True, vmem_limit_bytes=60 * 1024 * 1024
        ),
        name="attention_block",
    )(
        pages, prefix_id, lengths, prefix_len, pages, moves,
        queries, page_pool, prefix_cache.transpose(0, 2, 1), value_up, output_weight.T, residual,
    )
    new_pool = pl.pallas_call(
        place_pages,
        out_shape=jax.ShapeDtypeStruct((POOL, PAGE, LAT), bf),
        in_specs=[smem] * 2 + [hbm] * 2,
        out_specs=hbm,
        scratch_shapes=[
            vm((POOL, PAGE, LAT), bf), vm((2 * MOVES, PAGE, LAT), bf), pltpu.SemaphoreType.DMA((2 * PARTS + 1,))
        ],
        compiler_params=pltpu.CompilerParams(vmem_limit_bytes=60 * 1024 * 1024),
        name="place_pages",
    )(pages, moves, page_pool, come.reshape(2 * MOVES, PAGE, LAT))
    return (layer_out, new_pool)


def solution(mesh):
    in_specs = (
        P("dp", "tp", None),
        P("dp", None, None),
        P(),
        P("dp", None),
        P("dp"),
        P("dp"),
        P(),
        P("dp", None, None),
        P("tp", None, None),
        P("tp", "dp"),
        P("tp", "dp"),
    )
    out_specs = (P("tp", "dp"), P("dp", None, None))
    return jax.shard_map(local, mesh=mesh, in_specs=in_specs, out_specs=out_specs, check_vma=False)
```

```python
import functools

import jax
import jax.numpy as jnp
from jax import lax
from jax.experimental import pallas as pl
from jax.experimental.pallas import tpu as pltpu
from jax.sharding import PartitionSpec as P

MESH = pl.DeviceIdType.MESH

LAT = 576
KVL = 512
HEADS = 8
VH = 128
PAGE = 16
REQ = 96
MOVES = 32
CH = 32
CHUNKS = REQ // CH
ROWS = CH * HEADS
POOL = 192
PLEN = 384
NZ, NX, NY = 8, 4, 8
COLS = 224
DEPTH = HEADS * VH
SCALE = 192.0 ** (-0.5)
MASKED = -1e30

PLAN = (
    "p", "w", "a0", "b0", "h0", "r", "a1", "b1", "h1", "o", "r", "h0", "w", "r", "a2", "h1", "r", "w",
    "h0", "m0", "r", "b2", "h2", "s0", "h1", "m1", "h2", "s1", "s0", "n", "s1", "O", "h2", "m2", "s2",
    "s0", "s2", "s1", "s2",
)

NT = (((1,), (1,)), ((), ()))

W0 = 0
PD = W0 + 4
PY = PD + 8
PC = PY + 28
Z0 = PC + 8
CX = Z0 + 8 * CHUNKS
RS = CX + 2 * CHUNKS
RL = RS + 16 * CHUNKS
OR = RL + CHUNKS
SEMS = OR + 16


def div(a, n):
    return lax.div(a, jnp.int32(n))


def rem(a, n):
    return lax.rem(a, jnp.int32(n))


def fused(
    page_s, prefix_s, length_s, limit_s,
    page_r, move_r,
    q_h, pool_h, kt_h, vup_h, wt_h, res_h,
    out_ref, pool_o,
    q_v, big, kt_v, vup_v, w_v, res_v, order_v, order_r,
    table_v, table_s,
    stage, arr, q_f, keys, rowinfo, blend, stats, merged,
    zb, sx, rx, own, ss, rr, relay, red, new,
    lsem, ssem, rsem,
):
    d = lax.axis_index("dp")
    t = lax.axis_index("tp")
    z, x = div(d, NX), rem(d, NX)
    y, c = div(t, 2), rem(t, 2)
    kind, quarter = div(t, 4), rem(t, 4)

    def at_x(v):
        return (z * NX + rem(v + NX, NX), t)

    def at_z(v):
        return (rem(v + NZ, NZ) * NX + x, t)

    def at_y(v):
        return (d, rem(v + NY, NY) * 2 + c)

    def at_rank(v):
        return (rem(v + 32, 32), t)

    partner = (d, y * 2 + 1 - c)
    final_core = div(x, 2)
    diagonal = c == final_core

    sent = []

    def remote(src, dst, device, slot, recv_slot=None):
        return pltpu.make_async_remote_copy(
            src_ref=src, dst_ref=dst, send_sem=ssem.at[slot],
            recv_sem=rsem.at[slot if recv_slot is None else recv_slot],
            device_id=device, device_id_type=MESH,
        )

    def send(src, dst, device, slot):
        copy = remote(src, dst, device, slot)
        copy.start()
        sent.append(copy)

    def arrived(dst, slot):
        remote(dst, dst, partner, slot).wait_recv()

    def owner(core, e, s):
        return (z * NX + 2 * core + e, rem(y + s + NY, NY) * 2 + final_core)

    def itself(e):
        return diagonal & (2 * c + e == x)

    def order_itself(e):
        return (z == y) & (2 * c + e == x) & (rem(z, 2) == c)

    loads = {}
    for n, (name, src, dst) in enumerate([
        ("pool", pool_h, big.at[pl.ds(0, POOL)]), ("q", q_h, q_v), ("kt", kt_h, kt_v), ("vup", vup_h, vup_v),
        ("w", wt_h, w_v.at[x]), ("res", res_h, res_v),
    ]):
        loads[name] = pltpu.make_async_copy(src, dst, lsem.at[n])
        loads[name].start()

    barrier = pltpu.get_barrier_semaphore()

    def greet(device):
        pl.semaphore_signal(barrier, inc=1, device_id=device, device_id_type=MESH)

    for i in range(8):
        offset = kind + 4 * i
        if i == 0:
            @pl.when(offset != 0)
            def _():
                greet(at_rank(d - offset))
        else:
            greet(at_rank(d - offset))
    for device in (
        at_x(x + 1), at_x(x - 1), at_z(z + 1), at_z(z - 1), at_z(z + 2), at_z(z - 2),
        at_y(y + 1), at_y(y - 1), at_y(y + 2), partner,
    ):
        greet(device)
    for s in range(NY):
        for e in range(2):
            source = (z * NX + 2 * c + e, rem(y - s + NY, NY) * 2 + final_core)
            if s == 0:
                @pl.when(jnp.logical_not(itself(e)))
                def _():
                    greet(source)
            else:
                greet(source)
    for e in range(2):
        @pl.when(jnp.logical_not(order_itself(e)))
        def _():
            greet((y * NX + 2 * c + e, y * 2 + rem(z, 2)))

    def iota(shape, dim):
        return lax.broadcasted_iota(jnp.int32, shape, dim)

    def column_of(row, n):
        return jnp.sum(jnp.where(iota((n, n), 0) == iota((n, n), 1), row, 0), axis=1, keepdims=True)

    leaving = move_r[0]
    ahead_by = move_r[1] - d
    offsets = jnp.where(ahead_by < 0, ahead_by + 32, ahead_by)
    leaving_column = column_of(leaving, MOVES)
    offset_column = column_of(offsets, MOVES)
    is_left = iota((REQ, MOVES), 0) == leaving
    left = jnp.sum(jnp.where(is_left, 1, 0), axis=1, keepdims=True)
    move_of = jnp.sum(jnp.where(is_left, iota((REQ, MOVES), 1), 0), axis=1, keepdims=True)
    by_move = iota((MOVES, REQ), 1) == leaving_column
    left_row = jnp.sum(jnp.where(by_move, 1, 0), axis=0, keepdims=True)
    before = jnp.sum(
        jnp.where(iota((REQ, REQ), 1) < iota((REQ, REQ), 0), 1 - left_row, 0), axis=1, keepdims=True
    )
    position = jnp.where(left > 0, REQ - MOVES + move_of, before)
    placed = position == iota((REQ, 128), 1)
    order_v[...] = jnp.where(placed, 1.0, 0.0).astype(jnp.bfloat16)
    perm = jnp.sum(jnp.where(placed, iota((REQ, 128), 0), 0), axis=0, keepdims=True)
    table_v[0:1, :] = perm
    parity = lax.broadcasted_iota(jnp.int32, (MOVES, MOVES), 0) & 1
    sources = [0, 0]
    for p in range(2):
        row = page_r[p:p + 1, :]
        moved_page = jnp.sum(jnp.where(by_move, row, 0), axis=1, keepdims=True)
        for b in range(2):
            hit = (offset_column == iota((MOVES, MOVES), 1)) & (parity == b)
            table_v[1 + 2 * b + p:2 + 2 * b + p, :MOVES] = jnp.sum(
                jnp.where(hit, moved_page, 0), axis=0, keepdims=True
            )
        for half in range(2):
            sources[half] += jnp.sum(
                jnp.where(
                    moved_page == iota((MOVES, 128), 1) + 128 * half, POOL + 2 * iota((MOVES, 128), 0) + p, 0
                ),
                axis=0, keepdims=True,
            )
        b = lax.broadcasted_iota(jnp.int32, (1, MOVES), 1) & 1
        table_v[5 + p:6 + p, :MOVES] = (
            ((offsets & 3) * 4 + 2 * b + p) * 8 + lax.shift_right_logical(offsets, 2)
        )
    for half in range(2):
        table_v[8 + half:9 + half, :] = jnp.where(
            sources[half] > 0, sources[half], iota((1, 128), 1) + 128 * half
        )
    to_scalar = pltpu.make_async_copy(table_v, table_s, lsem.at[6])
    to_scalar.start()

    expected = 10 + jnp.where(kind == 0, 7, 8) + jnp.where(diagonal, 15, 16)
    expected = expected + jnp.where(z == y, jnp.where(diagonal & (rem(z, 2) == c), 15, 16), 0)
    pl.semaphore_wait(barrier, expected)
    to_scalar.wait()

    def listed(row, at, size):
        return jnp.clip(table_s[row, at], 0, size - 1)


    def weights():
        send(wt_h, w_v.at[x], at_x(x + 1), W0)
        send(wt_h, w_v.at[x], at_x(x - 1), W0 + 1)
        yield
        half = COLS // 2
        low, high = rem(x + NX - 1, NX), rem(x + 1, NX)
        arrived(w_v.at[low], W0)
        send(w_v.at[low, pl.ds(0, half)], w_v.at[low, pl.ds(0, half)], at_x(x + 1), W0 + 2)
        arrived(w_v.at[high], W0 + 1)
        send(w_v.at[high, pl.ds(half, half)], w_v.at[high, pl.ds(half, half)], at_x(x - 1), W0 + 3)
        yield
        far = rem(x + 2, NX)
        arrived(w_v.at[far, pl.ds(0, half)], W0 + 2)
        arrived(w_v.at[far, pl.ds(half, half)], W0 + 3)
        loads["w"].wait()
        yield

    def pages_out():
        loads["pool"].wait()
        for i in range(8):
            offset = kind + 4 * i
            stage[i] = big[listed(1 + quarter, offset, POOL)]

            def go():
                remote(stage.at[i], arr.at[t * 8 + i], at_rank(d + offset), PD + i).start()
            if i == 0:
                pl.when(offset != 0)(go)

                @pl.when(offset == 0)
                def _():
                    arr[t * 8] = jnp.zeros((PAGE, LAT), arr.dtype)
            else:
                go()
        yield

    def page_come(i):
        def come():
            copy = remote(stage.at[i], arr.at[t * 8 + i], partner, PD + i)
            copy.wait_send()
            copy.wait_recv()
        if i == 0:
            pl.when(kind != 0)(come)
        else:
            come()

    def pages_ring():
        parts = 4

        def part(o, k, core=c):
            return arr.at[pl.ds((o * 2 + core) * 8 + (8 // parts) * k, 8 // parts)]

        def block(o, core=c):
            return arr.at[pl.ds((o * 2 + core) * 8, 8)]

        devices = (at_y(y + 1), at_y(y - 1))
        for k in range(parts):
            for i in range(8 // parts):
                page_come(k * (8 // parts) + i)
            for way in range(2):
                send(part(y, k), part(y, k), devices[way], PY + 2 * k + way)
        send(block(y), block(y), partner, PC)
        yield
        for s in (1, 2, 3):
            sides = ((0, rem(y + NY - s, NY)), (1, rem(y + s, NY)))
            for k in range(parts):
                for way, o in sides:
                    slot = PY + 2 * parts * (s - 1) + 2 * k + way
                    arrived(part(o, k), slot)
                    if s < 3:
                        send(part(o, k), part(o, k), devices[way], slot + 2 * parts)
                    elif k // (parts // 2) == way:
                        send(part(o, k), part(o, k), devices[way], PY + 6 * parts + k)
            for way, o in sides:
                send(block(o), block(o), partner, PC + 2 * s - 1 + way)
            yield
        far = rem(y + 4, NY)
        for k in range(parts):
            arrived(part(far, k), PY + 6 * parts + k)
        send(block(far), block(far), partner, PC + 7)
        other = 1 - c
        arrived(block(y, other), PC)
        for s in (1, 2, 3):
            for way, o in ((0, rem(y + NY - s, NY)), (1, rem(y + s, NY))):
                arrived(block(o, other), PC + 2 * s - 1 + way)
        arrived(block(far, other), PC + 7)
        yield

    def prefix_part(n):
        if n == 0:
            loads["q"].wait()
            loads["kt"].wait()

        def place(j, _):
            slot = listed(0, n * CH + j, REQ)
            q_f[j] = q_v[slot].astype(jnp.float32)
            prefix = prefix_s[slot]
            rowinfo[0, j] = jnp.full((HEADS, 128), prefix, jnp.int32)
            rowinfo[1, j] = jnp.full((HEADS, 128), limit_s[prefix], jnp.int32)
            rowinfo[2, j] = jnp.full((HEADS, 128), length_s[slot], jnp.int32)
            return 0

        lax.fori_loop(0, CH, place, 0, unroll=4)
        q = q_f[...].reshape(ROWS, LAT).astype(jnp.bfloat16)
        which = rowinfo[0].reshape(ROWS, 128)[:, :1] == 0
        limit = rowinfo[1].reshape(ROWS, 128)[:, :1]
        scores = jnp.where(
            which,
            jnp.dot(q, kt_v[0], preferred_element_type=jnp.float32),
            jnp.dot(q, kt_v[1], preferred_element_type=jnp.float32),
        ) * SCALE
        column = lax.broadcasted_iota(jnp.int32, (ROWS, PLEN), 1)
        scores = jnp.where(column < limit, scores, MASKED)
        highest = jnp.max(scores, axis=1, keepdims=True)
        raised = jnp.exp(scores - highest)
        total = jnp.sum(raised, axis=1, keepdims=True)
        stats[0] = jnp.broadcast_to(highest, (ROWS, 128))
        stats[1] = jnp.broadcast_to(total, (ROWS, 128))
        blend[...] = lax.dot_general(
            jnp.where(which, raised, 0.0).astype(jnp.bfloat16), kt_v[0, :KVL, :], NT,
            preferred_element_type=jnp.float32,
        ) + lax.dot_general(
            jnp.where(which, 0.0, raised).astype(jnp.bfloat16), kt_v[1, :KVL, :], NT,
            preferred_element_type=jnp.float32,
        )

    def own_part(n):
        if n == 0:
            loads["vup"].wait()

        def place(j, _):
            if n < CHUNKS - 1:
                slot = listed(0, n * CH + j, REQ)
                keys[2 * j] = big[page_s[0, slot]]
                keys[2 * j + 1] = big[page_s[1, slot]]
            else:
                big[POOL + 2 * j] = arr[listed(5, j, 128)]
                big[POOL + 2 * j + 1] = arr[listed(6, j, 128)]
            return 0

        lax.fori_loop(0, CH, place, 0, unroll=4)
        group = 64
        row = lax.broadcasted_iota(jnp.int32, (group, 256), 0)
        column = lax.broadcasted_iota(jnp.int32, (group, 256), 1)
        same = lax.shift_right_logical(row, 3) == lax.shift_right_logical(column, 5)
        token = column & 31
        for g in range(ROWS // group):
            rows = pl.ds(g * group, group)
            q = q_f[pl.ds(g * 8, 8)].reshape(group, LAT).astype(jnp.bfloat16)
            pages = pl.ds(g * 16, 16) if n < CHUNKS - 1 else pl.ds(POOL + g * 16, 16)
            k = (keys if n < CHUNKS - 1 else big)[pages].reshape(256, LAT)
            length = rowinfo[2, pl.ds(g * 8, 8)].reshape(group, 128)[:, :1]
            scores = lax.dot_general(q, k, NT, preferred_element_type=jnp.float32) * SCALE
            scores = jnp.where(same & (token < length), scores, MASKED)
            high_own = jnp.max(scores, axis=1, keepdims=True)
            raised = jnp.exp(scores - high_own)
            total_own = jnp.sum(raised, axis=1, keepdims=True)
            blend_own = jnp.dot(
                raised.astype(jnp.bfloat16), k[:, :KVL], preferred_element_type=jnp.float32
            )
            high_pre = stats[0, rows, :][:, :1]
            total_pre = stats[1, rows, :][:, :1]
            ceiling = jnp.maximum(high_pre, high_own)
            f = jnp.exp(high_pre - ceiling)
            h = jnp.exp(high_own - ceiling)
            mixed = (f * blend[rows, :] + h * blend_own) / (f * total_pre + h * total_own)
            for l in range(KVL // 128):
                merged[l, rows, :] = mixed[:, l * 128:(l + 1) * 128]
        mine = pl.ds(pl.multiple_of(z * CH, CH), CH)
        for h in range(HEADS):
            a = jnp.concatenate(
                [merged[l, pl.ds(h, CH, stride=HEADS), :] for l in range(KVL // 128)], axis=1
            ).astype(jnp.bfloat16)
            zb[n, mine, h * VH:(h + 1) * VH] = jnp.dot(
                a, vup_v[h], preferred_element_type=jnp.float32
            ).astype(jnp.bfloat16)

    def new_pool():
        def place(i, row):
            new[128 * row + i] = big[listed(8 + row, i, POOL + 2 * MOVES)]
            return row

        for n, (row, count) in enumerate(((0, 128), (1, POOL - 128))):
            lax.fori_loop(0, count, place, row, unroll=4)
            part = pl.ds(128 * row, count)
            loads[f"new{row}"] = pltpu.make_async_copy(new.at[part], pool_o.at[part], lsem.at[7 + n])
            loads[f"new{row}"].start()

    def heads(n):
        def block(o):
            return zb.at[n, pl.ds(pl.multiple_of(o * CH, CH), CH)]

        def half(o, i):
            return zb.at[n, pl.ds(pl.multiple_of(o * CH + i * (CH // 2), CH // 2), CH // 2)]

        base = Z0 + 8 * n
        low = [rem(z + NZ - s, NZ) for s in range(4)]
        high = [rem(z + s, NZ) for s in range(5)]
        if n < CHUNKS - 1:
            send(block(z), block(z), at_z(z + 2), base + 2)
            send(block(z), block(z), at_z(z - 2), base + 3)
        else:
            first = [remote(block(z), block(z), at_z(z + 2 * w), base + 2 + (1 - w) // 2) for w in (1, -1)]
            for copy in first:
                copy.start()
            for copy in first:
                copy.wait_send()
        send(block(z), block(z), at_z(z + 1), base)
        send(block(z), block(z), at_z(z - 1), base + 1)
        yield
        arrived(block(low[2]), base + 2)
        send(half(low[2], 0), half(low[2], 0), at_z(z + 2), base + 6)
        send(block(low[2]), block(low[2]), at_z(z + 1), base + 4)
        arrived(block(high[2]), base + 3)
        send(half(high[2], 1), half(high[2], 1), at_z(z - 2), base + 7)
        send(block(high[2]), block(high[2]), at_z(z - 1), base + 5)
        yield
        arrived(block(low[1]), base)
        arrived(block(high[1]), base + 1)
        arrived(block(low[3]), base + 4)
        arrived(block(high[3]), base + 5)
        arrived(half(high[4], 0), base + 6)
        arrived(half(high[4], 1), base + 7)
        yield

    def product(n):
        for i in range(2):
            sx[n, i] = lax.dot_general(
                zb[n], w_v[2 * (1 - c) + i], NT, preferred_element_type=jnp.float32
            ).astype(jnp.bfloat16)
            send(sx.at[n, i], rx.at[n, i], partner, CX + 2 * n + i)
        for i in range(2):
            own[n, i] = lax.dot_general(zb[n], w_v[2 * c + i], NT, preferred_element_type=jnp.float32)

    def sums(n):
        base = RS + 16 * n

        @pl.when(rem(x, 2) == 1)
        def _():
            rr[n, 4] = jnp.zeros((2, CH, COLS), jnp.bfloat16)

        for i in range(2):
            arrived(rx.at[n, i], CX + 2 * n + i)
            ss[n, i] = (own[n, i] + rx[n, i].astype(jnp.float32)).astype(jnp.bfloat16)
        mine = rem(x, 2)

        def rows_of(s):
            return pl.ds(pl.multiple_of(rem(y + s, NY) * CH, CH), CH)

        def deliver(s, i):
            return remote(
                ss.at[n, i, rows_of(s)], rr.at[n, s, mine], owner(c, i, s), base + 2 * s + i, base + 2 * s + mine
            )

        send(ss.at[n, 1, rows_of(4)], relay.at[n], at_y(y - 2), RL + n)
        for s, i in ((4, 0), (3, 0), (3, 1), (5, 0), (5, 1), (2, 0), (2, 1), (6, 0), (1, 0), (1, 1), (7, 0), (7, 1)):
            copy = deliver(s, i)
            copy.start()
            sent.append(copy)
        for i in range(2):
            pl.when(jnp.logical_not(itself(i)))(deliver(0, i).start)

            @pl.when(itself(i))
            def _():
                rr[n, 0, mine] = ss[n, i, rows_of(0), :]
        yield
        arrived(relay.at[n], RL + n)
        ss[n, 1, rows_of(6)] = (
            ss[n, 1, rows_of(6), :].astype(jnp.float32) + relay[n].astype(jnp.float32)
        ).astype(jnp.bfloat16)
        copy = deliver(6, 1)
        copy.start()
        sent.append(copy)
        yield
        for e in range(2):
            total = None
            for s in (0, 1, 7, 2, 3, 5, 4, 6):
                copy = remote(rr.at[n, s, e], rr.at[n, s, e], partner, base + 2 * s + e)
                if s == 0:
                    pl.when(jnp.logical_not(itself(e)))(copy.wait_recv)
                elif s == 4:
                    pl.when(mine == 0)(copy.wait_recv)
                else:
                    copy.wait_recv()
                part = rr[n, s, e].astype(jnp.float32)
                total = part if total is None else total + part
            red[e, n * CH:(n + 1) * CH] = total
        rows = pl.ds(0, CH)
        for i in range(2):
            copy = remote(ss.at[n, i, rows], ss.at[n, i, rows], partner, base + i)
            pl.when(jnp.logical_not(itself(i)))(copy.wait_send)
        yield

    def order_copies(act):
        mine = rem(x, 2)
        for a in range(4):
            for column in range(NX):
                to = (2 * a + c) * NX + column
                copy = remote(
                    order_v, order_r.at[mine], (to, y * 2 + final_core), OR + 4 * a + column, OR + mine
                )
                pl.when((z == y) & jnp.logical_not(diagonal & (to == d)))(functools.partial(act, copy))

    def order_send():
        order_copies(lambda copy: copy.start())

        @pl.when((z == y) & diagonal & (rem(z, 2) == c))
        def _():
            order_r[rem(x, 2)] = order_v[...]

    def order_wait():
        order_copies(lambda copy: copy.wait_send())
        for e in range(2):
            copy = remote(order_v, order_r.at[e], partner, OR + e)
            pl.when(jnp.logical_not(order_itself(e)))(copy.wait_recv)

    def finish():
        loads["res"].wait()
        for e in range(2):
            place = order_r[e][:, :REQ]
            rows = pl.ds(e * REQ, REQ)
            total = red[e]
            high = total.astype(jnp.bfloat16)
            low = (total - high.astype(jnp.float32)).astype(jnp.bfloat16)
            placed = jnp.dot(place, high, preferred_element_type=jnp.float32) + jnp.dot(
                place, low, preferred_element_type=jnp.float32
            )
            out_ref[rows, :] = (res_v[rows, :].astype(jnp.float32) + placed).astype(jnp.bfloat16)

    running = {"p": pages_out(), "w": weights(), "r": pages_ring()}
    for n in range(CHUNKS):
        running[f"h{n}"] = heads(n)
        running[f"s{n}"] = sums(n)
    for step in PLAN:
        if step in running:
            next(running[step])
        elif step == "o":
            order_send()
        elif step == "O":
            order_wait()
        elif step == "n":
            new_pool()
        else:
            {"a": prefix_part, "b": own_part, "m": product}[step[0]](int(step[1]))
    finish()
    for copy in sent:
        copy.wait_send()
    loads["new0"].wait()
    loads["new1"].wait()


def local(
    queries, page_pool, prefix_cache, page_table, lengths, prefix_id, prefix_len,
    move_list, value_up, output_weight, residual,
):
    pages = page_table.T
    moves = move_list.transpose(2, 0, 1)
    smem = pl.BlockSpec(memory_space=pltpu.SMEM)
    vmem = pl.BlockSpec(memory_space=pltpu.VMEM)
    hbm = pl.BlockSpec(memory_space=pl.ANY)
    bf, f32 = jnp.bfloat16, jnp.float32
    vm = pltpu.VMEM
    layer_out, new_pool = pl.pallas_call(
        fused,
        out_shape=(
            jax.ShapeDtypeStruct((2 * REQ, COLS), bf),
            jax.ShapeDtypeStruct((POOL, PAGE, LAT), bf),
        ),
        in_specs=[smem] * 4 + [vmem] * 2 + [hbm] * 6,
        out_specs=(vmem, hbm),
        scratch_shapes=[
            vm((REQ, HEADS, LAT), bf), vm((POOL + 2 * MOVES, PAGE, LAT), bf), vm((2, LAT, PLEN), bf),
            vm((HEADS, KVL, VH), bf), vm((NX, COLS, DEPTH), bf), vm((2 * REQ, COLS), bf),
            vm((REQ, 128), bf), vm((2, REQ, 128), bf),
            vm((16, 128), jnp.int32), pltpu.SMEM((16, 128), jnp.int32),
            vm((8, PAGE, LAT), bf), vm((128, PAGE, LAT), bf), vm((CH, HEADS, LAT), f32),
            vm((2 * CH, PAGE, LAT), bf), vm((3, CH, HEADS, 128), jnp.int32), vm((ROWS, KVL), f32),
            vm((2, ROWS, 128), f32), vm((KVL // 128, ROWS, 128), f32),
            vm((CHUNKS, NZ * CH, DEPTH), bf), vm((CHUNKS, 2, NZ * CH, COLS), bf),
            vm((CHUNKS, 2, NZ * CH, COLS), bf), vm((CHUNKS, 2, NZ * CH, COLS), f32),
            vm((CHUNKS, 2, NZ * CH, COLS), bf), vm((CHUNKS, NY, 2, CH, COLS), bf),
            vm((CHUNKS, CH, COLS), bf), vm((2, REQ, COLS), f32), vm((POOL, PAGE, LAT), bf),
            pltpu.SemaphoreType.DMA((9,)),
            pltpu.SemaphoreType.DMA((SEMS,)),
            pltpu.SemaphoreType.DMA((SEMS,)),
        ],
        compiler_params=pltpu.CompilerParams(
            collective_id=0, has_side_effects=True, vmem_limit_bytes=60 * 1024 * 1024
        ),
        name="attention_block",
    )(
        pages, prefix_id, lengths, prefix_len, pages, moves,
        queries, page_pool, prefix_cache.transpose(0, 2, 1), value_up, output_weight.T, residual,
    )
    return (layer_out, new_pool)


def solution(mesh):
    in_specs = (
        P("dp", "tp", None),
        P("dp", None, None),
        P(),
        P("dp", None),
        P("dp"),
        P("dp"),
        P(),
        P("dp", None, None),
        P("tp", None, None),
        P("tp", "dp"),
        P("tp", "dp"),
    )
    out_specs = (P("tp", "dp"), P("dp", None, None))
    return jax.shard_map(local, mesh=mesh, in_specs=in_specs, out_specs=out_specs, check_vma=False)
```

```python
import functools

import jax
import jax.numpy as jnp
from jax import lax
from jax.experimental import pallas as pl
from jax.experimental.pallas import tpu as pltpu
from jax.sharding import PartitionSpec as P

MESH = pl.DeviceIdType.MESH

LAT = 576
KVL = 512
HEADS = 8
VH = 128
PAGE = 16
REQ = 96
MOVES = 32
CH = 32
CHUNKS = REQ // CH
ROWS = CH * HEADS
POOL = 192
PLEN = 384
NZ, NX, NY = 8, 4, 8
COLS = 224
DEPTH = HEADS * VH
SCALE = 192.0 ** (-0.5)
MASKED = -1e30

PLAN = (
    "p", "w", "a0", "b0", "h0", "r", "a1", "b1", "h1", "o", "r", "h0", "w", "r", "a2", "h1", "r", "w",
    "h0", "m0", "r", "b2", "h2", "s0", "h1", "m1", "h2", "s1", "s0", "n", "s1", "O", "h2", "m2", "s2",
    "s0", "s2", "s1", "s2",
)

NT = (((1,), (1,)), ((), ()))

W0 = 0
PD = W0 + 4
PY = PD + 8
PC = PY + 28
Z0 = PC + 8
CX = Z0 + 8 * CHUNKS
RS = CX + 2 * CHUNKS
RL = RS + 16 * CHUNKS
OR = RL + CHUNKS
SEMS = OR + 16


def div(a, n):
    return lax.div(a, jnp.int32(n))


def rem(a, n):
    return lax.rem(a, jnp.int32(n))


def fused(
    page_s, prefix_s, length_s, limit_s,
    page_r, move_r,
    q_h, pool_h, kt_h, vup_h, wt_h, res_h,
    out_ref, pool_o,
    q_v, big, kt_v, vup_v, w_v, res_v, order_v, order_r,
    table_v, table_s,
    stage, arr, q_f, keys, rowinfo, blend, stats, merged,
    zb, sx, rx, own, ss, rr, relay, red, new,
    lsem, ssem, rsem,
):
    d = lax.axis_index("dp")
    t = lax.axis_index("tp")
    z, x = div(d, NX), rem(d, NX)
    y, c = div(t, 2), rem(t, 2)
    kind, quarter = div(t, 4), rem(t, 4)

    def at_x(v):
        return (z * NX + rem(v + NX, NX), t)

    def at_z(v):
        return (rem(v + NZ, NZ) * NX + x, t)

    def at_y(v):
        return (d, rem(v + NY, NY) * 2 + c)

    def at_rank(v):
        return (rem(v + 32, 32), t)

    partner = (d, y * 2 + 1 - c)
    final_core = div(x, 2)
    diagonal = c == final_core

    sent = []

    def remote(src, dst, device, slot, recv_slot=None):
        return pltpu.make_async_remote_copy(
            src_ref=src, dst_ref=dst, send_sem=ssem.at[slot],
            recv_sem=rsem.at[slot if recv_slot is None else recv_slot],
            device_id=device, device_id_type=MESH,
        )

    def send(src, dst, device, slot):
        copy = remote(src, dst, device, slot)
        copy.start()
        sent.append(copy)

    def arrived(dst, slot):
        remote(dst, dst, partner, slot).wait_recv()

    def owner(core, e, s):
        return (z * NX + 2 * core + e, rem(y + s + NY, NY) * 2 + final_core)

    def itself(e):
        return diagonal & (2 * c + e == x)

    def order_itself(e):
        return (z == y) & (2 * c + e == x) & (rem(z, 2) == c)

    loads = {}
    for n, (name, src, dst) in enumerate([
        ("pool", pool_h, big.at[pl.ds(0, POOL)]), ("q", q_h, q_v), ("kt", kt_h, kt_v), ("vup", vup_h, vup_v),
        ("w", wt_h, w_v.at[x]), ("res", res_h, res_v),
    ]):
        loads[name] = pltpu.make_async_copy(src, dst, lsem.at[n])
        loads[name].start()

    barrier = pltpu.get_barrier_semaphore()

    def greet(device):
        pl.semaphore_signal(barrier, inc=1, device_id=device, device_id_type=MESH)

    for i in range(8):
        offset = kind + 4 * i
        if i == 0:
            @pl.when(offset != 0)
            def _():
                greet(at_rank(d - offset))
        else:
            greet(at_rank(d - offset))
    for device in (
        at_x(x + 1), at_x(x - 1), at_z(z + 1), at_z(z - 1), at_z(z + 2), at_z(z - 2),
        at_y(y + 1), at_y(y - 1), at_y(y + 2), partner,
    ):
        greet(device)
    for s in range(NY):
        for e in range(2):
            source = (z * NX + 2 * c + e, rem(y - s + NY, NY) * 2 + final_core)
            if s == 0:
                @pl.when(jnp.logical_not(itself(e)))
                def _():
                    greet(source)
            else:
                greet(source)
    for e in range(2):
        @pl.when(jnp.logical_not(order_itself(e)))
        def _():
            greet((y * NX + 2 * c + e, y * 2 + rem(z, 2)))

    def iota(shape, dim):
        return lax.broadcasted_iota(jnp.int32, shape, dim)

    def column_of(row, n):
        return jnp.sum(jnp.where(iota((n, n), 0) == iota((n, n), 1), row, 0), axis=1, keepdims=True)

    leaving = move_r[0]
    ahead_by = move_r[1] - d
    offsets = jnp.where(ahead_by < 0, ahead_by + 32, ahead_by)
    leaving_column = column_of(leaving, MOVES)
    offset_column = column_of(offsets, MOVES)
    is_left = iota((REQ, MOVES), 0) == leaving
    left = jnp.sum(jnp.where(is_left, 1, 0), axis=1, keepdims=True)
    move_of = jnp.sum(jnp.where(is_left, iota((REQ, MOVES), 1), 0), axis=1, keepdims=True)
    by_move = iota((MOVES, REQ), 1) == leaving_column
    left_row = jnp.sum(jnp.where(by_move, 1, 0), axis=0, keepdims=True)
    before = jnp.sum(
        jnp.where(iota((REQ, REQ), 1) < iota((REQ, REQ), 0), 1 - left_row, 0), axis=1, keepdims=True
    )
    position = jnp.where(left > 0, REQ - MOVES + move_of, before)
    placed = position == iota((REQ, 128), 1)
    order_v[...] = jnp.where(placed, 1.0, 0.0).astype(jnp.bfloat16)
    perm = jnp.sum(jnp.where(placed, iota((REQ, 128), 0), 0), axis=0, keepdims=True)
    table_v[0:1, :] = perm
    parity = lax.broadcasted_iota(jnp.int32, (MOVES, MOVES), 0) & 1
    sources = [0, 0]
    for p in range(2):
        row = page_r[p:p + 1, :]
        moved_page = jnp.sum(jnp.where(by_move, row, 0), axis=1, keepdims=True)
        for b in range(2):
            hit = (offset_column == iota((MOVES, MOVES), 1)) & (parity == b)
            table_v[1 + 2 * b + p:2 + 2 * b + p, :MOVES] = jnp.sum(
                jnp.where(hit, moved_page, 0), axis=0, keepdims=True
            )
        for half in range(2):
            sources[half] += jnp.sum(
                jnp.where(
                    moved_page == iota((MOVES, 128), 1) + 128 * half, POOL + 2 * iota((MOVES, 128), 0) + p, 0
                ),
                axis=0, keepdims=True,
            )
        b = lax.broadcasted_iota(jnp.int32, (1, MOVES), 1) & 1
        table_v[5 + p:6 + p, :MOVES] = (
            ((offsets & 3) * 4 + 2 * b + p) * 8 + lax.shift_right_logical(offsets, 2)
        )
    for half in range(2):
        table_v[8 + half:9 + half, :] = jnp.where(
            sources[half] > 0, sources[half], iota((1, 128), 1) + 128 * half
        )
    to_scalar = pltpu.make_async_copy(table_v, table_s, lsem.at[6])
    to_scalar.start()

    expected = 10 + jnp.where(kind == 0, 7, 8) + jnp.where(diagonal, 15, 16)
    expected = expected + jnp.where(z == y, jnp.where(diagonal & (rem(z, 2) == c), 15, 16), 0)
    pl.semaphore_wait(barrier, expected)
    to_scalar.wait()

    def listed(row, at, size):
        return jnp.clip(table_s[row, at], 0, size - 1)


    def weights():
        send(wt_h, w_v.at[x], at_x(x + 1), W0)
        send(wt_h, w_v.at[x], at_x(x - 1), W0 + 1)
        yield
        half = COLS // 2
        low, high = rem(x + NX - 1, NX), rem(x + 1, NX)
        arrived(w_v.at[low], W0)
        send(w_v.at[low, pl.ds(0, half)], w_v.at[low, pl.ds(0, half)], at_x(x + 1), W0 + 2)
        arrived(w_v.at[high], W0 + 1)
        send(w_v.at[high, pl.ds(half, half)], w_v.at[high, pl.ds(half, half)], at_x(x - 1), W0 + 3)
        yield
        far = rem(x + 2, NX)
        arrived(w_v.at[far, pl.ds(0, half)], W0 + 2)
        arrived(w_v.at[far, pl.ds(half, half)], W0 + 3)
        loads["w"].wait()
        yield

    def pages_out():
        loads["pool"].wait()
        for i in range(8):
            offset = kind + 4 * i
            stage[i] = big[listed(1 + quarter, offset, POOL)]

            def go():
                remote(stage.at[i], arr.at[t * 8 + i], at_rank(d + offset), PD + i).start()
            if i == 0:
                pl.when(offset != 0)(go)

                @pl.when(offset == 0)
                def _():
                    arr[t * 8] = jnp.zeros((PAGE, LAT), arr.dtype)
            else:
                go()
        yield

    def page_come(i):
        def come():
            copy = remote(stage.at[i], arr.at[t * 8 + i], partner, PD + i)
            copy.wait_send()
            copy.wait_recv()
        if i == 0:
            pl.when(kind != 0)(come)
        else:
            come()

    def pages_ring():
        parts = 4

        def part(o, k, core=c):
            return arr.at[pl.ds((o * 2 + core) * 8 + (8 // parts) * k, 8 // parts)]

        def block(o, core=c):
            return arr.at[pl.ds((o * 2 + core) * 8, 8)]

        devices = (at_y(y + 1), at_y(y - 1))
        for k in range(parts):
            for i in range(8 // parts):
                page_come(k * (8 // parts) + i)
            for way in range(2):
                send(part(y, k), part(y, k), devices[way], PY + 2 * k + way)
        send(block(y), block(y), partner, PC)
        yield
        for s in (1, 2, 3):
            sides = ((0, rem(y + NY - s, NY)), (1, rem(y + s, NY)))
            for k in range(parts):
                for way, o in sides:
                    slot = PY + 2 * parts * (s - 1) + 2 * k + way
                    arrived(part(o, k), slot)
                    if s < 3:
                        send(part(o, k), part(o, k), devices[way], slot + 2 * parts)
                    elif k // (parts // 2) == way:
                        send(part(o, k), part(o, k), devices[way], PY + 6 * parts + k)
            for way, o in sides:
                send(block(o), block(o), partner, PC + 2 * s - 1 + way)
            yield
        far = rem(y + 4, NY)
        for k in range(parts):
            arrived(part(far, k), PY + 6 * parts + k)
        send(block(far), block(far), partner, PC + 7)
        other = 1 - c
        arrived(block(y, other), PC)
        for s in (1, 2, 3):
            for way, o in ((0, rem(y + NY - s, NY)), (1, rem(y + s, NY))):
                arrived(block(o, other), PC + 2 * s - 1 + way)
        arrived(block(far, other), PC + 7)
        yield

    def prefix_part(n):
        if n == 0:
            loads["q"].wait()
            loads["kt"].wait()

        def place(j, _):
            slot = listed(0, n * CH + j, REQ)
            q_f[j] = q_v[slot].astype(jnp.float32)
            prefix = prefix_s[slot]
            rowinfo[0, j] = jnp.full((HEADS, 128), prefix, jnp.int32)
            rowinfo[1, j] = jnp.full((HEADS, 128), limit_s[prefix], jnp.int32)
            rowinfo[2, j] = jnp.full((HEADS, 128), length_s[slot], jnp.int32)
            return 0

        lax.fori_loop(0, CH, place, 0, unroll=4)
        q = q_f[...].reshape(ROWS, LAT).astype(jnp.bfloat16)
        which = rowinfo[0].reshape(ROWS, 128)[:, :1] == 0
        limit = rowinfo[1].reshape(ROWS, 128)[:, :1]
        scores = jnp.where(
            which,
            jnp.dot(q, kt_v[0], preferred_element_type=jnp.float32),
            jnp.dot(q, kt_v[1], preferred_element_type=jnp.float32),
        ) * SCALE
        column = lax.broadcasted_iota(jnp.int32, (ROWS, PLEN), 1)
        scores = jnp.where(column < limit, scores, MASKED)
        highest = jnp.max(scores, axis=1, keepdims=True)
        raised = jnp.exp(scores - highest)
        total = jnp.sum(raised, axis=1, keepdims=True)
        stats[0] = jnp.broadcast_to(highest, (ROWS, 128))
        stats[1] = jnp.broadcast_to(total, (ROWS, 128))
        blend[...] = lax.dot_general(
            jnp.where(which, raised, 0.0).astype(jnp.bfloat16), kt_v[0, :KVL, :], NT,
            preferred_element_type=jnp.float32,
        ) + lax.dot_general(
            jnp.where(which, 0.0, raised).astype(jnp.bfloat16), kt_v[1, :KVL, :], NT,
            preferred_element_type=jnp.float32,
        )

    def own_part(n):
        if n == 0:
            loads["vup"].wait()

        def place(j, _):
            if n < CHUNKS - 1:
                slot = listed(0, n * CH + j, REQ)
                keys[2 * j] = big[page_s[0, slot]]
                keys[2 * j + 1] = big[page_s[1, slot]]
            else:
                big[POOL + 2 * j] = arr[listed(5, j, 128)]
                big[POOL + 2 * j + 1] = arr[listed(6, j, 128)]
            return 0

        lax.fori_loop(0, CH, place, 0, unroll=4)
        group = 64
        row = lax.broadcasted_iota(jnp.int32, (group, 256), 0)
        column = lax.broadcasted_iota(jnp.int32, (group, 256), 1)
        same = lax.shift_right_logical(row, 3) == lax.shift_right_logical(column, 5)
        token = column & 31
        for g in range(ROWS // group):
            rows = pl.ds(g * group, group)
            q = q_f[pl.ds(g * 8, 8)].reshape(group, LAT).astype(jnp.bfloat16)
            pages = pl.ds(g * 16, 16) if n < CHUNKS - 1 else pl.ds(POOL + g * 16, 16)
            k = (keys if n < CHUNKS - 1 else big)[pages].reshape(256, LAT)
            length = rowinfo[2, pl.ds(g * 8, 8)].reshape(group, 128)[:, :1]
            scores = lax.dot_general(q, k, NT, preferred_element_type=jnp.float32) * SCALE
            scores = jnp.where(same & (token < length), scores, MASKED)
            high_own = jnp.max(scores, axis=1, keepdims=True)
            raised = jnp.exp(scores - high_own)
            total_own = jnp.sum(raised, axis=1, keepdims=True)
            blend_own = jnp.dot(
                raised.astype(jnp.bfloat16), k[:, :KVL], preferred_element_type=jnp.float32
            )
            high_pre = stats[0, rows, :][:, :1]
            total_pre = stats[1, rows, :][:, :1]
            ceiling = jnp.maximum(high_pre, high_own)
            f = jnp.exp(high_pre - ceiling)
            h = jnp.exp(high_own - ceiling)
            mixed = (f * blend[rows, :] + h * blend_own) / (f * total_pre + h * total_own)
            for l in range(KVL // 128):
                merged[l, rows, :] = mixed[:, l * 128:(l + 1) * 128]
        mine = pl.ds(pl.multiple_of(z * CH, CH), CH)
        for h in range(HEADS):
            a = jnp.concatenate(
                [merged[l, pl.ds(h, CH, stride=HEADS), :] for l in range(KVL // 128)], axis=1
            ).astype(jnp.bfloat16)
            zb[n, mine, h * VH:(h + 1) * VH] = jnp.dot(
                a, vup_v[h], preferred_element_type=jnp.float32
            ).astype(jnp.bfloat16)

    def new_pool():
        def place(i, row):
            new[128 * row + i] = big[listed(8 + row, i, POOL + 2 * MOVES)]
            return row

        for n, (row, count) in enumerate(((0, 128), (1, POOL - 128))):
            lax.fori_loop(0, count, place, row, unroll=4)
            part = pl.ds(128 * row, count)
            loads[f"new{row}"] = pltpu.make_async_copy(new.at[part], pool_o.at[part], lsem.at[7 + n])
            loads[f"new{row}"].start()

    def heads(n):
        def block(o):
            return zb.at[n, pl.ds(pl.multiple_of(o * CH, CH), CH)]

        def half(o, i):
            return zb.at[n, pl.ds(pl.multiple_of(o * CH + i * (CH // 2), CH // 2), CH // 2)]

        base = Z0 + 8 * n
        low = [rem(z + NZ - s, NZ) for s in range(4)]
        high = [rem(z + s, NZ) for s in range(5)]
        if n < CHUNKS - 1:
            send(block(z), block(z), at_z(z + 2), base + 2)
            send(block(z), block(z), at_z(z - 2), base + 3)
        else:
            first = [remote(block(z), block(z), at_z(z + 2 * w), base + 2 + (1 - w) // 2) for w in (1, -1)]
            for copy in first:
                copy.start()
            for copy in first:
                copy.wait_send()
        send(block(z), block(z), at_z(z + 1), base)
        send(block(z), block(z), at_z(z - 1), base + 1)
        yield
        arrived(block(low[2]), base + 2)
        send(half(low[2], 0), half(low[2], 0), at_z(z + 2), base + 6)
        send(block(low[2]), block(low[2]), at_z(z + 1), base + 4)
        arrived(block(high[2]), base + 3)
        send(half(high[2], 1), half(high[2], 1), at_z(z - 2), base + 7)
        send(block(high[2]), block(high[2]), at_z(z - 1), base + 5)
        yield
        arrived(block(low[1]), base)
        arrived(block(high[1]), base + 1)
        arrived(block(low[3]), base + 4)
        arrived(block(high[3]), base + 5)
        arrived(half(high[4], 0), base + 6)
        arrived(half(high[4], 1), base + 7)
        yield

    def product(n):
        for i in range(2):
            sx[n, i] = lax.dot_general(
                zb[n], w_v[2 * (1 - c) + i], NT, preferred_element_type=jnp.float32
            ).astype(jnp.bfloat16)
            send(sx.at[n, i], rx.at[n, i], partner, CX + 2 * n + i)
        for i in range(2):
            own[n, i] = lax.dot_general(zb[n], w_v[2 * c + i], NT, preferred_element_type=jnp.float32)

    def sums(n):
        base = RS + 16 * n

        @pl.when(rem(x, 2) == 1)
        def _():
            rr[n, 4] = jnp.zeros((2, CH, COLS), jnp.bfloat16)

        for i in range(2):
            arrived(rx.at[n, i], CX + 2 * n + i)
            ss[n, i] = (own[n, i] + rx[n, i].astype(jnp.float32)).astype(jnp.bfloat16)
        mine = rem(x, 2)

        def rows_of(s):
            return pl.ds(pl.multiple_of(rem(y + s, NY) * CH, CH), CH)

        def deliver(s, i):
            return remote(
                ss.at[n, i, rows_of(s)], rr.at[n, s, mine], owner(c, i, s), base + 2 * s + i, base + 2 * s + mine
            )

        send(ss.at[n, 1, rows_of(4)], relay.at[n], at_y(y - 2), RL + n)
        for s, i in ((4, 0), (3, 0), (3, 1), (5, 0), (5, 1), (2, 0), (2, 1), (6, 0), (1, 0), (1, 1), (7, 0), (7, 1)):
            copy = deliver(s, i)
            copy.start()
            sent.append(copy)
        for i in range(2):
            pl.when(jnp.logical_not(itself(i)))(deliver(0, i).start)

            @pl.when(itself(i))
            def _():
                rr[n, 0, mine] = ss[n, i, rows_of(0), :]
        yield
        arrived(relay.at[n], RL + n)
        ss[n, 1, rows_of(6)] = (
            ss[n, 1, rows_of(6), :].astype(jnp.float32) + relay[n].astype(jnp.float32)
        ).astype(jnp.bfloat16)
        copy = deliver(6, 1)
        copy.start()
        sent.append(copy)
        yield
        for e in range(2):
            total = None
            for s in (0, 1, 7, 2, 3, 5, 4, 6):
                copy = remote(rr.at[n, s, e], rr.at[n, s, e], partner, base + 2 * s + e)
                if s == 0:
                    pl.when(jnp.logical_not(itself(e)))(copy.wait_recv)
                elif s == 4:
                    pl.when(mine == 0)(copy.wait_recv)
                else:
                    copy.wait_recv()
                part = rr[n, s, e].astype(jnp.float32)
                total = part if total is None else total + part
            red[e, n * CH:(n + 1) * CH] = total
        rows = pl.ds(0, CH)
        for i in range(2):
            copy = remote(ss.at[n, i, rows], ss.at[n, i, rows], partner, base + i)
            pl.when(jnp.logical_not(itself(i)))(copy.wait_send)
        yield

    def order_copies(act):
        mine = rem(x, 2)
        for a in range(4):
            for column in range(NX):
                to = (2 * a + c) * NX + column
                copy = remote(
                    order_v, order_r.at[mine], (to, y * 2 + final_core), OR + 4 * a + column, OR + mine
                )
                pl.when((z == y) & jnp.logical_not(diagonal & (to == d)))(functools.partial(act, copy))

    def order_send():
        order_copies(lambda copy: copy.start())

        @pl.when((z == y) & diagonal & (rem(z, 2) == c))
        def _():
            order_r[rem(x, 2)] = order_v[...]

    def order_wait():
        order_copies(lambda copy: copy.wait_send())
        for e in range(2):
            copy = remote(order_v, order_r.at[e], partner, OR + e)
            pl.when(jnp.logical_not(order_itself(e)))(copy.wait_recv)

    def finish():
        loads["res"].wait()
        for e in range(2):
            place = order_r[e][:, :REQ]
            rows = pl.ds(e * REQ, REQ)
            total = red[e]
            high = total.astype(jnp.bfloat16)
            low = (total - high.astype(jnp.float32)).astype(jnp.bfloat16)
            placed = jnp.dot(place, high, preferred_element_type=jnp.float32) + jnp.dot(
                place, low, preferred_element_type=jnp.float32
            )
            out_ref[rows, :] = (res_v[rows, :].astype(jnp.float32) + placed).astype(jnp.bfloat16)

    running = {"p": pages_out(), "w": weights(), "r": pages_ring()}
    for n in range(CHUNKS):
        running[f"h{n}"] = heads(n)
        running[f"s{n}"] = sums(n)
    for step in PLAN:
        if step in running:
            next(running[step])
        elif step == "o":
            order_send()
        elif step == "O":
            order_wait()
        elif step == "n":
            new_pool()
        else:
            {"a": prefix_part, "b": own_part, "m": product}[step[0]](int(step[1]))
    finish()
    for copy in sent:
        copy.wait_send()
    loads["new0"].wait()
    loads["new1"].wait()


PARTS = 4


def settle(pool_h, layer_h, pool_o, layer_o, pool_v, layer_v, sem):
    parts = [pl.ds(n * (POOL // PARTS), POOL // PARTS) for n in range(PARTS)]
    loads = [pltpu.make_async_copy(pool_h.at[part], pool_v.at[part], sem.at[n]) for n, part in enumerate(parts)]
    stores = [pltpu.make_async_copy(pool_v.at[part], pool_o.at[part], sem.at[PARTS + n]) for n, part in enumerate(parts)]
    load = pltpu.make_async_copy(layer_h, layer_v, sem.at[2 * PARTS])
    store = pltpu.make_async_copy(layer_v, layer_o, sem.at[2 * PARTS + 1])
    for copy in loads:
        copy.start()
    load.start()
    for n in range(PARTS):
        loads[n].wait()
        stores[n].start()
    load.wait()
    store.start()
    for copy in stores:
        copy.wait()
    store.wait()


def local(
    queries, page_pool, prefix_cache, page_table, lengths, prefix_id, prefix_len,
    move_list, value_up, output_weight, residual,
):
    pages = page_table.T
    moves = move_list.transpose(2, 0, 1)
    smem = pl.BlockSpec(memory_space=pltpu.SMEM)
    vmem = pl.BlockSpec(memory_space=pltpu.VMEM)
    hbm = pl.BlockSpec(memory_space=pl.ANY)
    bf, f32 = jnp.bfloat16, jnp.float32
    vm = pltpu.VMEM
    layer_out, new_pool = pl.pallas_call(
        fused,
        out_shape=(
            jax.ShapeDtypeStruct((2 * REQ, COLS), bf),
            jax.ShapeDtypeStruct((POOL, PAGE, LAT), bf),
        ),
        in_specs=[smem] * 4 + [vmem] * 2 + [hbm] * 6,
        out_specs=(vmem, hbm),
        scratch_shapes=[
            vm((REQ, HEADS, LAT), bf), vm((POOL + 2 * MOVES, PAGE, LAT), bf), vm((2, LAT, PLEN), bf),
            vm((HEADS, KVL, VH), bf), vm((NX, COLS, DEPTH), bf), vm((2 * REQ, COLS), bf),
            vm((REQ, 128), bf), vm((2, REQ, 128), bf),
            vm((16, 128), jnp.int32), pltpu.SMEM((16, 128), jnp.int32),
            vm((8, PAGE, LAT), bf), vm((128, PAGE, LAT), bf), vm((CH, HEADS, LAT), f32),
            vm((2 * CH, PAGE, LAT), bf), vm((3, CH, HEADS, 128), jnp.int32), vm((ROWS, KVL), f32),
            vm((2, ROWS, 128), f32), vm((KVL // 128, ROWS, 128), f32),
            vm((CHUNKS, NZ * CH, DEPTH), bf), vm((CHUNKS, 2, NZ * CH, COLS), bf),
            vm((CHUNKS, 2, NZ * CH, COLS), bf), vm((CHUNKS, 2, NZ * CH, COLS), f32),
            vm((CHUNKS, 2, NZ * CH, COLS), bf), vm((CHUNKS, NY, 2, CH, COLS), bf),
            vm((CHUNKS, CH, COLS), bf), vm((2, REQ, COLS), f32), vm((POOL, PAGE, LAT), bf),
            pltpu.SemaphoreType.DMA((9,)),
            pltpu.SemaphoreType.DMA((SEMS,)),
            pltpu.SemaphoreType.DMA((SEMS,)),
        ],
        compiler_params=pltpu.CompilerParams(
            collective_id=0, has_side_effects=True, vmem_limit_bytes=60 * 1024 * 1024
        ),
        name="attention_block",
    )(
        pages, prefix_id, lengths, prefix_len, pages, moves,
        queries, page_pool, prefix_cache.transpose(0, 2, 1), value_up, output_weight.T, residual,
    )
    new_pool, layer_out = pl.pallas_call(
        settle,
        out_shape=(jax.ShapeDtypeStruct(new_pool.shape, bf), jax.ShapeDtypeStruct(layer_out.shape, bf)),
        in_specs=[hbm] * 2,
        out_specs=(hbm, hbm),
        scratch_shapes=[
            vm(new_pool.shape, bf), vm(layer_out.shape, bf), pltpu.SemaphoreType.DMA((2 * PARTS + 2,))
        ],
        compiler_params=pltpu.CompilerParams(vmem_limit_bytes=60 * 1024 * 1024),
        name="settle",
    )(new_pool, layer_out)
    return (layer_out, new_pool)


def solution(mesh):
    in_specs = (
        P("dp", "tp", None),
        P("dp", None, None),
        P(),
        P("dp", None),
        P("dp"),
        P("dp"),
        P(),
        P("dp", None, None),
        P("tp", None, None),
        P("tp", "dp"),
        P("tp", "dp"),
    )
    out_specs = (P("tp", "dp"), P("dp", None, None))
    return jax.shard_map(local, mesh=mesh, in_specs=in_specs, out_specs=out_specs, check_vma=False)
```

```python
import functools

import jax
import jax.numpy as jnp
from jax import lax
from jax.experimental import pallas as pl
from jax.experimental.pallas import tpu as pltpu
from jax.sharding import PartitionSpec as P

MESH = pl.DeviceIdType.MESH

LAT = 576
KVL = 512
HEADS = 8
VH = 128
PAGE = 16
REQ = 96
MOVES = 32
CH = 32
CHUNKS = REQ // CH
ROWS = CH * HEADS
POOL = 192
PLEN = 384
NZ, NX, NY = 8, 4, 8
COLS = 224
DEPTH = HEADS * VH
SCALE = 192.0 ** (-0.5)
MASKED = -1e30

PLAN = (
    "p", "w", "a0", "b0", "h0", "r", "a1", "b1", "h1", "o", "r", "h0", "w", "r", "a2", "h1", "r", "w",
    "h0", "m0", "r", "b2", "h2", "s0", "h1", "m1", "h2", "s1", "s0", "n", "s1", "O", "h2", "m2", "k", "s2",
    "d", "s0", "s2", "s1", "s2",
)

NT = (((1,), (1,)), ((), ()))

W0 = 0
PD = W0 + 4
PY = PD + 8
PC = PY + 28
Z0 = PC + 8
CX = Z0 + 8 * CHUNKS
RS = CX + 2 * CHUNKS
RL = RS + 16 * CHUNKS
OR = RL + CHUNKS
SEMS = OR + 16


def div(a, n):
    return lax.div(a, jnp.int32(n))


def rem(a, n):
    return lax.rem(a, jnp.int32(n))


def fused(
    page_s, prefix_s, length_s, limit_s,
    page_r, move_r,
    q_h, pool_h, kt_h, vup_h, wt_h, res_h,
    out_ref, pool_o,
    q_v, big, kt_v, vup_v, w_v, res_v, order_v, order_r,
    table_v, table_s,
    stage, arr, q_f, keys, rowinfo, blend, stats, merged,
    zb, sx, rx, own, ss, rr, relay, red, new,
    lsem, ssem, rsem,
):
    d = lax.axis_index("dp")
    t = lax.axis_index("tp")
    z, x = div(d, NX), rem(d, NX)
    y, c = div(t, 2), rem(t, 2)
    kind, quarter = div(t, 4), rem(t, 4)

    def at_x(v):
        return (z * NX + rem(v + NX, NX), t)

    def at_z(v):
        return (rem(v + NZ, NZ) * NX + x, t)

    def at_y(v):
        return (d, rem(v + NY, NY) * 2 + c)

    def at_rank(v):
        return (rem(v + 32, 32), t)

    partner = (d, y * 2 + 1 - c)
    final_core = div(x, 2)
    diagonal = c == final_core

    sent = []

    def remote(src, dst, device, slot, recv_slot=None):
        return pltpu.make_async_remote_copy(
            src_ref=src, dst_ref=dst, send_sem=ssem.at[slot],
            recv_sem=rsem.at[slot if recv_slot is None else recv_slot],
            device_id=device, device_id_type=MESH,
        )

    def send(src, dst, device, slot):
        copy = remote(src, dst, device, slot)
        copy.start()
        sent.append(copy)

    def arrived(dst, slot):
        remote(dst, dst, partner, slot).wait_recv()

    def owner(core, e, s):
        return (z * NX + 2 * core + e, rem(y + s + NY, NY) * 2 + final_core)

    def itself(e):
        return diagonal & (2 * c + e == x)

    def order_itself(e):
        return (z == y) & (2 * c + e == x) & (rem(z, 2) == c)

    loads = {}
    for n, (name, src, dst) in enumerate([
        ("pool", pool_h, big.at[pl.ds(0, POOL)]), ("q", q_h, q_v), ("kt", kt_h, kt_v), ("vup", vup_h, vup_v),
        ("w", wt_h, w_v.at[x]), ("res", res_h, res_v),
    ]):
        loads[name] = pltpu.make_async_copy(src, dst, lsem.at[n])
        loads[name].start()

    barrier = pltpu.get_barrier_semaphore()

    def greet(device):
        pl.semaphore_signal(barrier, inc=1, device_id=device, device_id_type=MESH)

    for i in range(8):
        offset = kind + 4 * i
        if i == 0:
            @pl.when(offset != 0)
            def _():
                greet(at_rank(d - offset))
        else:
            greet(at_rank(d - offset))
    for device in (
        at_x(x + 1), at_x(x - 1), at_z(z + 1), at_z(z - 1), at_z(z + 2), at_z(z - 2),
        at_y(y + 1), at_y(y - 1), at_y(y + 2), partner,
    ):
        greet(device)
    for s in range(NY):
        for e in range(2):
            source = (z * NX + 2 * c + e, rem(y - s + NY, NY) * 2 + final_core)
            if s == 0:
                @pl.when(jnp.logical_not(itself(e)))
                def _():
                    greet(source)
            else:
                greet(source)
    for e in range(2):
        @pl.when(jnp.logical_not(order_itself(e)))
        def _():
            greet((y * NX + 2 * c + e, y * 2 + rem(z, 2)))

    def iota(shape, dim):
        return lax.broadcasted_iota(jnp.int32, shape, dim)

    def column_of(row, n):
        return jnp.sum(jnp.where(iota((n, n), 0) == iota((n, n), 1), row, 0), axis=1, keepdims=True)

    leaving = move_r[0]
    ahead_by = move_r[1] - d
    offsets = jnp.where(ahead_by < 0, ahead_by + 32, ahead_by)
    leaving_column = column_of(leaving, MOVES)
    offset_column = column_of(offsets, MOVES)
    is_left = iota((REQ, MOVES), 0) == leaving
    left = jnp.sum(jnp.where(is_left, 1, 0), axis=1, keepdims=True)
    move_of = jnp.sum(jnp.where(is_left, iota((REQ, MOVES), 1), 0), axis=1, keepdims=True)
    by_move = iota((MOVES, REQ), 1) == leaving_column
    left_row = jnp.sum(jnp.where(by_move, 1, 0), axis=0, keepdims=True)
    before = jnp.sum(
        jnp.where(iota((REQ, REQ), 1) < iota((REQ, REQ), 0), 1 - left_row, 0), axis=1, keepdims=True
    )
    position = jnp.where(left > 0, REQ - MOVES + move_of, before)
    placed = position == iota((REQ, 128), 1)
    order_v[...] = jnp.where(placed, 1.0, 0.0).astype(jnp.bfloat16)
    perm = jnp.sum(jnp.where(placed, iota((REQ, 128), 0), 0), axis=0, keepdims=True)
    table_v[0:1, :] = perm
    parity = lax.broadcasted_iota(jnp.int32, (MOVES, MOVES), 0) & 1
    sources = [0, 0]
    for p in range(2):
        row = page_r[p:p + 1, :]
        moved_page = jnp.sum(jnp.where(by_move, row, 0), axis=1, keepdims=True)
        for b in range(2):
            hit = (offset_column == iota((MOVES, MOVES), 1)) & (parity == b)
            table_v[1 + 2 * b + p:2 + 2 * b + p, :MOVES] = jnp.sum(
                jnp.where(hit, moved_page, 0), axis=0, keepdims=True
            )
        for half in range(2):
            sources[half] += jnp.sum(
                jnp.where(
                    moved_page == iota((MOVES, 128), 1) + 128 * half, POOL + 2 * iota((MOVES, 128), 0) + p, 0
                ),
                axis=0, keepdims=True,
            )
        b = lax.broadcasted_iota(jnp.int32, (1, MOVES), 1) & 1
        table_v[5 + p:6 + p, :MOVES] = (
            ((offsets & 3) * 4 + 2 * b + p) * 8 + lax.shift_right_logical(offsets, 2)
        )
    for half in range(2):
        table_v[8 + half:9 + half, :] = jnp.where(
            sources[half] > 0, sources[half], iota((1, 128), 1) + 128 * half
        )
    to_scalar = pltpu.make_async_copy(table_v, table_s, lsem.at[6])
    to_scalar.start()

    expected = 10 + jnp.where(kind == 0, 7, 8) + jnp.where(diagonal, 15, 16)
    expected = expected + jnp.where(z == y, jnp.where(diagonal & (rem(z, 2) == c), 15, 16), 0)
    pl.semaphore_wait(barrier, expected)
    to_scalar.wait()

    def listed(row, at, size):
        return jnp.clip(table_s[row, at], 0, size - 1)


    def weights():
        send(wt_h, w_v.at[x], at_x(x + 1), W0)
        send(wt_h, w_v.at[x], at_x(x - 1), W0 + 1)
        yield
        half = COLS // 2
        low, high = rem(x + NX - 1, NX), rem(x + 1, NX)
        arrived(w_v.at[low], W0)
        send(w_v.at[low, pl.ds(0, half)], w_v.at[low, pl.ds(0, half)], at_x(x + 1), W0 + 2)
        arrived(w_v.at[high], W0 + 1)
        send(w_v.at[high, pl.ds(half, half)], w_v.at[high, pl.ds(half, half)], at_x(x - 1), W0 + 3)
        yield
        far = rem(x + 2, NX)
        arrived(w_v.at[far, pl.ds(0, half)], W0 + 2)
        arrived(w_v.at[far, pl.ds(half, half)], W0 + 3)
        loads["w"].wait()
        yield

    def pages_out():
        loads["pool"].wait()
        for i in range(8):
            offset = kind + 4 * i
            stage[i] = big[listed(1 + quarter, offset, POOL)]

            def go():
                remote(stage.at[i], arr.at[t * 8 + i], at_rank(d + offset), PD + i).start()
            if i == 0:
                pl.when(offset != 0)(go)

                @pl.when(offset == 0)
                def _():
                    arr[t * 8] = jnp.zeros((PAGE, LAT), arr.dtype)
            else:
                go()
        yield

    def page_come(i):
        def come():
            copy = remote(stage.at[i], arr.at[t * 8 + i], partner, PD + i)
            copy.wait_send()
            copy.wait_recv()
        if i == 0:
            pl.when(kind != 0)(come)
        else:
            come()

    def pages_ring():
        parts = 4

        def part(o, k, core=c):
            return arr.at[pl.ds((o * 2 + core) * 8 + (8 // parts) * k, 8 // parts)]

        def block(o, core=c):
            return arr.at[pl.ds((o * 2 + core) * 8, 8)]

        devices = (at_y(y + 1), at_y(y - 1))
        for k in range(parts):
            for i in range(8 // parts):
                page_come(k * (8 // parts) + i)
            for way in range(2):
                send(part(y, k), part(y, k), devices[way], PY + 2 * k + way)
        send(block(y), block(y), partner, PC)
        yield
        for s in (1, 2, 3):
            sides = ((0, rem(y + NY - s, NY)), (1, rem(y + s, NY)))
            for k in range(parts):
                for way, o in sides:
                    slot = PY + 2 * parts * (s - 1) + 2 * k + way
                    arrived(part(o, k), slot)
                    if s < 3:
                        send(part(o, k), part(o, k), devices[way], slot + 2 * parts)
                    elif k // (parts // 2) == way:
                        send(part(o, k), part(o, k), devices[way], PY + 6 * parts + k)
            for way, o in sides:
                send(block(o), block(o), partner, PC + 2 * s - 1 + way)
            yield
        far = rem(y + 4, NY)
        for k in range(parts):
            arrived(part(far, k), PY + 6 * parts + k)
        send(block(far), block(far), partner, PC + 7)
        other = 1 - c
        arrived(block(y, other), PC)
        for s in (1, 2, 3):
            for way, o in ((0, rem(y + NY - s, NY)), (1, rem(y + s, NY))):
                arrived(block(o, other), PC + 2 * s - 1 + way)
        arrived(block(far, other), PC + 7)
        yield

    def prefix_part(n):
        if n == 0:
            loads["q"].wait()
            loads["kt"].wait()

        def place(j, _):
            slot = listed(0, n * CH + j, REQ)
            q_f[j] = q_v[slot].astype(jnp.float32)
            prefix = prefix_s[slot]
            rowinfo[0, j] = jnp.full((HEADS, 128), prefix, jnp.int32)
            rowinfo[1, j] = jnp.full((HEADS, 128), limit_s[prefix], jnp.int32)
            rowinfo[2, j] = jnp.full((HEADS, 128), length_s[slot], jnp.int32)
            return 0

        lax.fori_loop(0, CH, place, 0, unroll=4)
        q = q_f[...].reshape(ROWS, LAT).astype(jnp.bfloat16)
        which = rowinfo[0].reshape(ROWS, 128)[:, :1] == 0
        limit = rowinfo[1].reshape(ROWS, 128)[:, :1]
        scores = jnp.where(
            which,
            jnp.dot(q, kt_v[0], preferred_element_type=jnp.float32),
            jnp.dot(q, kt_v[1], preferred_element_type=jnp.float32),
        ) * SCALE
        column = lax.broadcasted_iota(jnp.int32, (ROWS, PLEN), 1)
        scores = jnp.where(column < limit, scores, MASKED)
        highest = jnp.max(scores, axis=1, keepdims=True)
        raised = jnp.exp(scores - highest)
        total = jnp.sum(raised, axis=1, keepdims=True)
        stats[0] = jnp.broadcast_to(highest, (ROWS, 128))
        stats[1] = jnp.broadcast_to(total, (ROWS, 128))
        blend[...] = lax.dot_general(
            jnp.where(which, raised, 0.0).astype(jnp.bfloat16), kt_v[0, :KVL, :], NT,
            preferred_element_type=jnp.float32,
        ) + lax.dot_general(
            jnp.where(which, 0.0, raised).astype(jnp.bfloat16), kt_v[1, :KVL, :], NT,
            preferred_element_type=jnp.float32,
        )

    def own_part(n):
        if n == 0:
            loads["vup"].wait()

        def place(j, _):
            if n < CHUNKS - 1:
                slot = listed(0, n * CH + j, REQ)
                keys[2 * j] = big[page_s[0, slot]]
                keys[2 * j + 1] = big[page_s[1, slot]]
            else:
                big[POOL + 2 * j] = arr[listed(5, j, 128)]
                big[POOL + 2 * j + 1] = arr[listed(6, j, 128)]
            return 0

        lax.fori_loop(0, CH, place, 0, unroll=4)
        group = 64
        row = lax.broadcasted_iota(jnp.int32, (group, 256), 0)
        column = lax.broadcasted_iota(jnp.int32, (group, 256), 1)
        same = lax.shift_right_logical(row, 3) == lax.shift_right_logical(column, 5)
        token = column & 31
        for g in range(ROWS // group):
            rows = pl.ds(g * group, group)
            q = q_f[pl.ds(g * 8, 8)].reshape(group, LAT).astype(jnp.bfloat16)
            pages = pl.ds(g * 16, 16) if n < CHUNKS - 1 else pl.ds(POOL + g * 16, 16)
            k = (keys if n < CHUNKS - 1 else big)[pages].reshape(256, LAT)
            length = rowinfo[2, pl.ds(g * 8, 8)].reshape(group, 128)[:, :1]
            scores = lax.dot_general(q, k, NT, preferred_element_type=jnp.float32) * SCALE
            scores = jnp.where(same & (token < length), scores, MASKED)
            high_own = jnp.max(scores, axis=1, keepdims=True)
            raised = jnp.exp(scores - high_own)
            total_own = jnp.sum(raised, axis=1, keepdims=True)
            blend_own = jnp.dot(
                raised.astype(jnp.bfloat16), k[:, :KVL], preferred_element_type=jnp.float32
            )
            high_pre = stats[0, rows, :][:, :1]
            total_pre = stats[1, rows, :][:, :1]
            ceiling = jnp.maximum(high_pre, high_own)
            f = jnp.exp(high_pre - ceiling)
            h = jnp.exp(high_own - ceiling)
            mixed = (f * blend[rows, :] + h * blend_own) / (f * total_pre + h * total_own)
            for l in range(KVL // 128):
                merged[l, rows, :] = mixed[:, l * 128:(l + 1) * 128]
        mine = pl.ds(pl.multiple_of(z * CH, CH), CH)
        for h in range(HEADS):
            a = jnp.concatenate(
                [merged[l, pl.ds(h, CH, stride=HEADS), :] for l in range(KVL // 128)], axis=1
            ).astype(jnp.bfloat16)
            zb[n, mine, h * VH:(h + 1) * VH] = jnp.dot(
                a, vup_v[h], preferred_element_type=jnp.float32
            ).astype(jnp.bfloat16)

    def new_pool():
        def place(i, row):
            new[128 * row + i] = big[listed(8 + row, i, POOL + 2 * MOVES)]
            return row

        for n, (row, count) in enumerate(((0, 128), (1, POOL - 128))):
            lax.fori_loop(0, count, place, row, unroll=4)
            part = pl.ds(128 * row, count)
            loads[f"new{row}"] = pltpu.make_async_copy(new.at[part], pool_o.at[part], lsem.at[7 + n])
            loads[f"new{row}"].start()

    def heads(n):
        def block(o):
            return zb.at[n, pl.ds(pl.multiple_of(o * CH, CH), CH)]

        def half(o, i):
            return zb.at[n, pl.ds(pl.multiple_of(o * CH + i * (CH // 2), CH // 2), CH // 2)]

        base = Z0 + 8 * n
        low = [rem(z + NZ - s, NZ) for s in range(4)]
        high = [rem(z + s, NZ) for s in range(5)]
        if n < CHUNKS - 1:
            send(block(z), block(z), at_z(z + 2), base + 2)
            send(block(z), block(z), at_z(z - 2), base + 3)
        else:
            first = [remote(block(z), block(z), at_z(z + 2 * w), base + 2 + (1 - w) // 2) for w in (1, -1)]
            for copy in first:
                copy.start()
            for copy in first:
                copy.wait_send()
        send(block(z), block(z), at_z(z + 1), base)
        send(block(z), block(z), at_z(z - 1), base + 1)
        yield
        arrived(block(low[2]), base + 2)
        send(half(low[2], 0), half(low[2], 0), at_z(z + 2), base + 6)
        send(block(low[2]), block(low[2]), at_z(z + 1), base + 4)
        arrived(block(high[2]), base + 3)
        send(half(high[2], 1), half(high[2], 1), at_z(z - 2), base + 7)
        send(block(high[2]), block(high[2]), at_z(z - 1), base + 5)
        yield
        arrived(block(low[1]), base)
        arrived(block(high[1]), base + 1)
        arrived(block(low[3]), base + 4)
        arrived(block(high[3]), base + 5)
        arrived(half(high[4], 0), base + 6)
        arrived(half(high[4], 1), base + 7)
        yield

    def product(n):
        for i in range(2):
            sx[n, i] = lax.dot_general(
                zb[n], w_v[2 * (1 - c) + i], NT, preferred_element_type=jnp.float32
            ).astype(jnp.bfloat16)
            send(sx.at[n, i], rx.at[n, i], partner, CX + 2 * n + i)
        for i in range(2):
            own[n, i] = lax.dot_general(zb[n], w_v[2 * c + i], NT, preferred_element_type=jnp.float32)

    def sums(n):
        base = RS + 16 * n

        @pl.when(rem(x, 2) == 1)
        def _():
            rr[n, 4] = jnp.zeros((2, CH, COLS), jnp.bfloat16)

        for i in range(2):
            arrived(rx.at[n, i], CX + 2 * n + i)
            ss[n, i] = (own[n, i] + rx[n, i].astype(jnp.float32)).astype(jnp.bfloat16)
        mine = rem(x, 2)

        def rows_of(s):
            return pl.ds(pl.multiple_of(rem(y + s, NY) * CH, CH), CH)

        def deliver(s, i):
            return remote(
                ss.at[n, i, rows_of(s)], rr.at[n, s, mine], owner(c, i, s), base + 2 * s + i, base + 2 * s + mine
            )

        send(ss.at[n, 1, rows_of(4)], relay.at[n], at_y(y - 2), RL + n)
        for s, i in ((4, 0), (3, 0), (3, 1), (5, 0), (5, 1), (2, 0), (2, 1), (6, 0), (1, 0), (1, 1), (7, 0), (7, 1)):
            copy = deliver(s, i)
            copy.start()
            sent.append(copy)
        for i in range(2):
            pl.when(jnp.logical_not(itself(i)))(deliver(0, i).start)

            @pl.when(itself(i))
            def _():
                rr[n, 0, mine] = ss[n, i, rows_of(0), :]
        yield
        arrived(relay.at[n], RL + n)
        ss[n, 1, rows_of(6)] = (
            ss[n, 1, rows_of(6), :].astype(jnp.float32) + relay[n].astype(jnp.float32)
        ).astype(jnp.bfloat16)
        copy = deliver(6, 1)
        copy.start()
        sent.append(copy)
        yield
        for e in range(2):
            total = None
            for s in (0, 1, 7, 2, 3, 5, 4, 6):
                copy = remote(rr.at[n, s, e], rr.at[n, s, e], partner, base + 2 * s + e)
                if s == 0:
                    pl.when(jnp.logical_not(itself(e)))(copy.wait_recv)
                elif s == 4:
                    pl.when(mine == 0)(copy.wait_recv)
                else:
                    copy.wait_recv()
                part = rr[n, s, e].astype(jnp.float32)
                total = part if total is None else total + part
            red[e, n * CH:(n + 1) * CH] = total
        rows = pl.ds(0, CH)
        for i in range(2):
            copy = remote(ss.at[n, i, rows], ss.at[n, i, rows], partner, base + i)
            pl.when(jnp.logical_not(itself(i)))(copy.wait_send)
        yield

    def order_copies(act):
        mine = rem(x, 2)
        for a in range(4):
            for column in range(NX):
                to = (2 * a + c) * NX + column
                copy = remote(
                    order_v, order_r.at[mine], (to, y * 2 + final_core), OR + 4 * a + column, OR + mine
                )
                pl.when((z == y) & jnp.logical_not(diagonal & (to == d)))(functools.partial(act, copy))

    def order_send():
        order_copies(lambda copy: copy.start())

        @pl.when((z == y) & diagonal & (rem(z, 2) == c))
        def _():
            order_r[rem(x, 2)] = order_v[...]

    def order_wait():
        order_copies(lambda copy: copy.wait_send())
        for e in range(2):
            copy = remote(order_v, order_r.at[e], partner, OR + e)
            pl.when(jnp.logical_not(order_itself(e)))(copy.wait_recv)

    def finish():
        loads["res"].wait()
        for e in range(2):
            place = order_r[e][:, :REQ]
            rows = pl.ds(e * REQ, REQ)
            total = red[e]
            high = total.astype(jnp.bfloat16)
            low = (total - high.astype(jnp.float32)).astype(jnp.bfloat16)
            placed = jnp.dot(place, high, preferred_element_type=jnp.float32) + jnp.dot(
                place, low, preferred_element_type=jnp.float32
            )
            out_ref[rows, :] = (res_v[rows, :].astype(jnp.float32) + placed).astype(jnp.bfloat16)

    running = {"p": pages_out(), "w": weights(), "r": pages_ring()}
    for n in range(CHUNKS):
        running[f"h{n}"] = heads(n)
        running[f"s{n}"] = sums(n)
    for step in PLAN:
        if step in running:
            next(running[step])
        elif step == "o":
            order_send()
        elif step == "O":
            order_wait()
        elif step == "n":
            new_pool()
        elif step == "k":
            older = sent[:]
            del sent[:]
        elif step == "d":
            for copy in older:
                copy.wait_send()
        else:
            {"a": prefix_part, "b": own_part, "m": product}[step[0]](int(step[1]))
    finish()
    for copy in sent:
        copy.wait_send()
    loads["new0"].wait()
    loads["new1"].wait()


PARTS = 4


def settle(pool_h, layer_h, pool_o, layer_o, pool_v, layer_v, sem):
    parts = [pl.ds(n * (POOL // PARTS), POOL // PARTS) for n in range(PARTS)]
    loads = [pltpu.make_async_copy(pool_h.at[part], pool_v.at[part], sem.at[n]) for n, part in enumerate(parts)]
    stores = [pltpu.make_async_copy(pool_v.at[part], pool_o.at[part], sem.at[PARTS + n]) for n, part in enumerate(parts)]
    load = pltpu.make_async_copy(layer_h, layer_v, sem.at[2 * PARTS])
    store = pltpu.make_async_copy(layer_v, layer_o, sem.at[2 * PARTS + 1])
    for copy in loads:
        copy.start()
    load.start()
    for n in range(PARTS):
        loads[n].wait()
        stores[n].start()
    load.wait()
    store.start()
    for copy in stores:
        copy.wait()
    store.wait()


def local(
    queries, page_pool, prefix_cache, page_table, lengths, prefix_id, prefix_len,
    move_list, value_up, output_weight, residual,
):
    pages = page_table.T
    moves = move_list.transpose(2, 0, 1)
    smem = pl.BlockSpec(memory_space=pltpu.SMEM)
    vmem = pl.BlockSpec(memory_space=pltpu.VMEM)
    hbm = pl.BlockSpec(memory_space=pl.ANY)
    bf, f32 = jnp.bfloat16, jnp.float32
    vm = pltpu.VMEM
    layer_out, new_pool = pl.pallas_call(
        fused,
        out_shape=(
            jax.ShapeDtypeStruct((2 * REQ, COLS), bf),
            jax.ShapeDtypeStruct((POOL, PAGE, LAT), bf),
        ),
        in_specs=[smem] * 4 + [vmem] * 2 + [hbm] * 6,
        out_specs=(vmem, hbm),
        scratch_shapes=[
            vm((REQ, HEADS, LAT), bf), vm((POOL + 2 * MOVES, PAGE, LAT), bf), vm((2, LAT, PLEN), bf),
            vm((HEADS, KVL, VH), bf), vm((NX, COLS, DEPTH), bf), vm((2 * REQ, COLS), bf),
            vm((REQ, 128), bf), vm((2, REQ, 128), bf),
            vm((16, 128), jnp.int32), pltpu.SMEM((16, 128), jnp.int32),
            vm((8, PAGE, LAT), bf), vm((128, PAGE, LAT), bf), vm((CH, HEADS, LAT), f32),
            vm((2 * CH, PAGE, LAT), bf), vm((3, CH, HEADS, 128), jnp.int32), vm((ROWS, KVL), f32),
            vm((2, ROWS, 128), f32), vm((KVL // 128, ROWS, 128), f32),
            vm((CHUNKS, NZ * CH, DEPTH), bf), vm((CHUNKS, 2, NZ * CH, COLS), bf),
            vm((CHUNKS, 2, NZ * CH, COLS), bf), vm((CHUNKS, 2, NZ * CH, COLS), f32),
            vm((CHUNKS, 2, NZ * CH, COLS), bf), vm((CHUNKS, NY, 2, CH, COLS), bf),
            vm((CHUNKS, CH, COLS), bf), vm((2, REQ, COLS), f32), vm((POOL, PAGE, LAT), bf),
            pltpu.SemaphoreType.DMA((9,)),
            pltpu.SemaphoreType.DMA((SEMS,)),
            pltpu.SemaphoreType.DMA((SEMS,)),
        ],
        compiler_params=pltpu.CompilerParams(
            collective_id=0, has_side_effects=True, vmem_limit_bytes=60 * 1024 * 1024
        ),
        name="attention_block",
    )(
        pages, prefix_id, lengths, prefix_len, pages, moves,
        queries, page_pool, prefix_cache.transpose(0, 2, 1), value_up, output_weight.T, residual,
    )
    new_pool, layer_out = pl.pallas_call(
        settle,
        out_shape=(jax.ShapeDtypeStruct(new_pool.shape, bf), jax.ShapeDtypeStruct(layer_out.shape, bf)),
        in_specs=[hbm] * 2,
        out_specs=(hbm, hbm),
        scratch_shapes=[
            vm(new_pool.shape, bf), vm(layer_out.shape, bf), pltpu.SemaphoreType.DMA((2 * PARTS + 2,))
        ],
        compiler_params=pltpu.CompilerParams(vmem_limit_bytes=60 * 1024 * 1024),
        name="settle",
    )(new_pool, layer_out)
    return (layer_out, new_pool)


def solution(mesh):
    in_specs = (
        P("dp", "tp", None),
        P("dp", None, None),
        P(),
        P("dp", None),
        P("dp"),
        P("dp"),
        P(),
        P("dp", None, None),
        P("tp", None, None),
        P("tp", "dp"),
        P("tp", "dp"),
    )
    out_specs = (P("tp", "dp"), P("dp", None, None))
    return jax.shard_map(local, mesh=mesh, in_specs=in_specs, out_specs=out_specs, check_vma=False)
```

```python
import functools

import jax
import jax.numpy as jnp
from jax import lax
from jax.experimental import pallas as pl
from jax.experimental.pallas import tpu as pltpu
from jax.sharding import PartitionSpec as P

MESH = pl.DeviceIdType.MESH

LAT = 576
KVL = 512
HEADS = 8
VH = 128
PAGE = 16
REQ = 96
MOVES = 32
CH = 32
CHUNKS = REQ // CH
ROWS = CH * HEADS
POOL = 192
PLEN = 384
NZ, NX, NY = 8, 4, 8
COLS = 224
DEPTH = HEADS * VH
SCALE = 192.0 ** (-0.5)
MASKED = -1e30

PLAN = (
    "p", "w", "a0", "b0", "h0", "r", "a1", "b1", "h1", "o", "r", "h0", "w", "r", "a2", "h1", "r", "w",
    "h0", "m0", "r", "b2", "h2", "s0", "h1", "m1", "h2", "s1", "s0", "n", "s1", "O", "h2", "m2", "s2",
    "s0", "s2", "s1", "s2",
)

NT = (((1,), (1,)), ((), ()))

W0 = 0
PD = W0 + 4
PY = PD + 8
PC = PY + 56
Z0 = PC + 8
CX = Z0 + 8 * CHUNKS
RS = CX + 2 * CHUNKS
RL = RS + 16 * CHUNKS
OR = RL + CHUNKS
SEMS = OR + 16


def div(a, n):
    return lax.div(a, jnp.int32(n))


def rem(a, n):
    return lax.rem(a, jnp.int32(n))


def fused(
    page_s, prefix_s, length_s, limit_s,
    page_r, move_r,
    q_h, pool_h, kt_h, vup_h, wt_h, res_h,
    out_ref, pool_o,
    q_v, big, kt_v, vup_v, w_v, res_v, order_v, order_r,
    table_v, table_s,
    stage, arr, q_f, keys, rowinfo, blend, stats, merged,
    zb, sx, rx, own, ss, rr, relay, red, new,
    lsem, ssem, rsem,
):
    d = lax.axis_index("dp")
    t = lax.axis_index("tp")
    z, x = div(d, NX), rem(d, NX)
    y, c = div(t, 2), rem(t, 2)
    kind, quarter = div(t, 4), rem(t, 4)

    def at_x(v):
        return (z * NX + rem(v + NX, NX), t)

    def at_z(v):
        return (rem(v + NZ, NZ) * NX + x, t)

    def at_y(v):
        return (d, rem(v + NY, NY) * 2 + c)

    def at_rank(v):
        return (rem(v + 32, 32), t)

    partner = (d, y * 2 + 1 - c)
    final_core = div(x, 2)
    diagonal = c == final_core

    sent = []

    def remote(src, dst, device, slot, recv_slot=None):
        return pltpu.make_async_remote_copy(
            src_ref=src, dst_ref=dst, send_sem=ssem.at[slot],
            recv_sem=rsem.at[slot if recv_slot is None else recv_slot],
            device_id=device, device_id_type=MESH,
        )

    def send(src, dst, device, slot):
        copy = remote(src, dst, device, slot)
        copy.start()
        sent.append(copy)

    def arrived(dst, slot):
        remote(dst, dst, partner, slot).wait_recv()

    def owner(core, e, s):
        return (z * NX + 2 * core + e, rem(y + s + NY, NY) * 2 + final_core)

    def itself(e):
        return diagonal & (2 * c + e == x)

    def order_itself(e):
        return (z == y) & (2 * c + e == x) & (rem(z, 2) == c)

    loads = {}
    for n, (name, src, dst) in enumerate([
        ("pool", pool_h, big.at[pl.ds(0, POOL)]), ("q", q_h, q_v), ("kt", kt_h, kt_v), ("vup", vup_h, vup_v),
        ("w", wt_h, w_v.at[x]), ("res", res_h, res_v),
    ]):
        loads[name] = pltpu.make_async_copy(src, dst, lsem.at[n])
        loads[name].start()

    barrier = pltpu.get_barrier_semaphore()

    def greet(device):
        pl.semaphore_signal(barrier, inc=1, device_id=device, device_id_type=MESH)

    for i in range(8):
        offset = kind + 4 * i
        if i == 0:
            @pl.when(offset != 0)
            def _():
                greet(at_rank(d - offset))
        else:
            greet(at_rank(d - offset))
    for device in (
        at_x(x + 1), at_x(x - 1), at_z(z + 1), at_z(z - 1), at_z(z + 2), at_z(z - 2),
        at_y(y + 1), at_y(y - 1), at_y(y + 2), partner,
    ):
        greet(device)
    for s in range(NY):
        for e in range(2):
            source = (z * NX + 2 * c + e, rem(y - s + NY, NY) * 2 + final_core)
            if s == 0:
                @pl.when(jnp.logical_not(itself(e)))
                def _():
                    greet(source)
            else:
                greet(source)
    for e in range(2):
        @pl.when(jnp.logical_not(order_itself(e)))
        def _():
            greet((y * NX + 2 * c + e, y * 2 + rem(z, 2)))

    def iota(shape, dim):
        return lax.broadcasted_iota(jnp.int32, shape, dim)

    def column_of(row, n):
        return jnp.sum(jnp.where(iota((n, n), 0) == iota((n, n), 1), row, 0), axis=1, keepdims=True)

    leaving = move_r[0]
    ahead_by = move_r[1] - d
    offsets = jnp.where(ahead_by < 0, ahead_by + 32, ahead_by)
    leaving_column = column_of(leaving, MOVES)
    offset_column = column_of(offsets, MOVES)
    is_left = iota((REQ, MOVES), 0) == leaving
    left = jnp.sum(jnp.where(is_left, 1, 0), axis=1, keepdims=True)
    move_of = jnp.sum(jnp.where(is_left, iota((REQ, MOVES), 1), 0), axis=1, keepdims=True)
    by_move = iota((MOVES, REQ), 1) == leaving_column
    left_row = jnp.sum(jnp.where(by_move, 1, 0), axis=0, keepdims=True)
    before = jnp.sum(
        jnp.where(iota((REQ, REQ), 1) < iota((REQ, REQ), 0), 1 - left_row, 0), axis=1, keepdims=True
    )
    position = jnp.where(left > 0, REQ - MOVES + move_of, before)
    placed = position == iota((REQ, 128), 1)
    order_v[...] = jnp.where(placed, 1.0, 0.0).astype(jnp.bfloat16)
    perm = jnp.sum(jnp.where(placed, iota((REQ, 128), 0), 0), axis=0, keepdims=True)
    table_v[0:1, :] = perm
    parity = lax.broadcasted_iota(jnp.int32, (MOVES, MOVES), 0) & 1
    sources = [0, 0]
    for p in range(2):
        row = page_r[p:p + 1, :]
        moved_page = jnp.sum(jnp.where(by_move, row, 0), axis=1, keepdims=True)
        for b in range(2):
            hit = (offset_column == iota((MOVES, MOVES), 1)) & (parity == b)
            table_v[1 + 2 * b + p:2 + 2 * b + p, :MOVES] = jnp.sum(
                jnp.where(hit, moved_page, 0), axis=0, keepdims=True
            )
        for half in range(2):
            sources[half] += jnp.sum(
                jnp.where(
                    moved_page == iota((MOVES, 128), 1) + 128 * half, POOL + 2 * iota((MOVES, 128), 0) + p, 0
                ),
                axis=0, keepdims=True,
            )
        b = lax.broadcasted_iota(jnp.int32, (1, MOVES), 1) & 1
        table_v[5 + p:6 + p, :MOVES] = (
            ((offsets & 3) * 4 + 2 * b + p) * 8 + lax.shift_right_logical(offsets, 2)
        )
    for half in range(2):
        table_v[8 + half:9 + half, :] = jnp.where(
            sources[half] > 0, sources[half], iota((1, 128), 1) + 128 * half
        )
    to_scalar = pltpu.make_async_copy(table_v, table_s, lsem.at[6])
    to_scalar.start()

    expected = 10 + jnp.where(kind == 0, 7, 8) + jnp.where(diagonal, 15, 16)
    expected = expected + jnp.where(z == y, jnp.where(diagonal & (rem(z, 2) == c), 15, 16), 0)
    pl.semaphore_wait(barrier, expected)
    to_scalar.wait()

    def listed(row, at, size):
        return jnp.clip(table_s[row, at], 0, size - 1)


    def weights():
        send(wt_h, w_v.at[x], at_x(x + 1), W0)
        send(wt_h, w_v.at[x], at_x(x - 1), W0 + 1)
        yield
        half = COLS // 2
        low, high = rem(x + NX - 1, NX), rem(x + 1, NX)
        arrived(w_v.at[low], W0)
        send(w_v.at[low, pl.ds(0, half)], w_v.at[low, pl.ds(0, half)], at_x(x + 1), W0 + 2)
        arrived(w_v.at[high], W0 + 1)
        send(w_v.at[high, pl.ds(half, half)], w_v.at[high, pl.ds(half, half)], at_x(x - 1), W0 + 3)
        yield
        far = rem(x + 2, NX)
        arrived(w_v.at[far, pl.ds(0, half)], W0 + 2)
        arrived(w_v.at[far, pl.ds(half, half)], W0 + 3)
        loads["w"].wait()
        yield

    def pages_out():
        loads["pool"].wait()
        for i in range(8):
            offset = kind + 4 * i
            stage[i] = big[listed(1 + quarter, offset, POOL)]

            def go():
                remote(stage.at[i], arr.at[t * 8 + i], at_rank(d + offset), PD + i).start()
            if i == 0:
                pl.when(offset != 0)(go)

                @pl.when(offset == 0)
                def _():
                    arr[t * 8] = jnp.zeros((PAGE, LAT), arr.dtype)
            else:
                go()
        yield

    def page_come(i):
        def come():
            copy = remote(stage.at[i], arr.at[t * 8 + i], partner, PD + i)
            copy.wait_send()
            copy.wait_recv()
        if i == 0:
            pl.when(kind != 0)(come)
        else:
            come()

    def pages_ring():
        parts = 8

        def part(o, k, core=c):
            return arr.at[pl.ds((o * 2 + core) * 8 + (8 // parts) * k, 8 // parts)]

        def block(o, core=c):
            return arr.at[pl.ds((o * 2 + core) * 8, 8)]

        devices = (at_y(y + 1), at_y(y - 1))
        for k in range(parts):
            for i in range(8 // parts):
                page_come(k * (8 // parts) + i)
            for way in range(2):
                send(part(y, k), part(y, k), devices[way], PY + 2 * k + way)
        send(block(y), block(y), partner, PC)
        yield
        for s in (1, 2, 3):
            sides = ((0, rem(y + NY - s, NY)), (1, rem(y + s, NY)))
            for k in range(parts):
                for way, o in sides:
                    slot = PY + 2 * parts * (s - 1) + 2 * k + way
                    arrived(part(o, k), slot)
                    if s < 3:
                        send(part(o, k), part(o, k), devices[way], slot + 2 * parts)
                    elif k // (parts // 2) == way:
                        send(part(o, k), part(o, k), devices[way], PY + 6 * parts + k)
            for way, o in sides:
                send(block(o), block(o), partner, PC + 2 * s - 1 + way)
            yield
        far = rem(y + 4, NY)
        for k in range(parts):
            arrived(part(far, k), PY + 6 * parts + k)
        send(block(far), block(far), partner, PC + 7)
        other = 1 - c
        arrived(block(y, other), PC)
        for s in (1, 2, 3):
            for way, o in ((0, rem(y + NY - s, NY)), (1, rem(y + s, NY))):
                arrived(block(o, other), PC + 2 * s - 1 + way)
        arrived(block(far, other), PC + 7)
        yield

    def prefix_part(n):
        if n == 0:
            loads["q"].wait()
            loads["kt"].wait()

        def place(j, _):
            slot = listed(0, n * CH + j, REQ)
            q_f[j] = q_v[slot].astype(jnp.float32)
            prefix = prefix_s[slot]
            rowinfo[0, j] = jnp.full((HEADS, 128), prefix, jnp.int32)
            rowinfo[1, j] = jnp.full((HEADS, 128), limit_s[prefix], jnp.int32)
            rowinfo[2, j] = jnp.full((HEADS, 128), length_s[slot], jnp.int32)
            return 0

        lax.fori_loop(0, CH, place, 0, unroll=4)
        q = q_f[...].reshape(ROWS, LAT).astype(jnp.bfloat16)
        which = rowinfo[0].reshape(ROWS, 128)[:, :1] == 0
        limit = rowinfo[1].reshape(ROWS, 128)[:, :1]
        scores = jnp.where(
            which,
            jnp.dot(q, kt_v[0], preferred_element_type=jnp.float32),
            jnp.dot(q, kt_v[1], preferred_element_type=jnp.float32),
        ) * SCALE
        column = lax.broadcasted_iota(jnp.int32, (ROWS, PLEN), 1)
        scores = jnp.where(column < limit, scores, MASKED)
        highest = jnp.max(scores, axis=1, keepdims=True)
        raised = jnp.exp(scores - highest)
        total = jnp.sum(raised, axis=1, keepdims=True)
        stats[0] = jnp.broadcast_to(highest, (ROWS, 128))
        stats[1] = jnp.broadcast_to(total, (ROWS, 128))
        blend[...] = lax.dot_general(
            jnp.where(which, raised, 0.0).astype(jnp.bfloat16), kt_v[0, :KVL, :], NT,
            preferred_element_type=jnp.float32,
        ) + lax.dot_general(
            jnp.where(which, 0.0, raised).astype(jnp.bfloat16), kt_v[1, :KVL, :], NT,
            preferred_element_type=jnp.float32,
        )

    def own_part(n):
        if n == 0:
            loads["vup"].wait()

        def place(j, _):
            if n < CHUNKS - 1:
                slot = listed(0, n * CH + j, REQ)
                keys[2 * j] = big[page_s[0, slot]]
                keys[2 * j + 1] = big[page_s[1, slot]]
            else:
                big[POOL + 2 * j] = arr[listed(5, j, 128)]
                big[POOL + 2 * j + 1] = arr[listed(6, j, 128)]
            return 0

        lax.fori_loop(0, CH, place, 0, unroll=4)
        group = 64
        row = lax.broadcasted_iota(jnp.int32, (group, 256), 0)
        column = lax.broadcasted_iota(jnp.int32, (group, 256), 1)
        same = lax.shift_right_logical(row, 3) == lax.shift_right_logical(column, 5)
        token = column & 31
        for g in range(ROWS // group):
            rows = pl.ds(g * group, group)
            q = q_f[pl.ds(g * 8, 8)].reshape(group, LAT).astype(jnp.bfloat16)
            pages = pl.ds(g * 16, 16) if n < CHUNKS - 1 else pl.ds(POOL + g * 16, 16)
            k = (keys if n < CHUNKS - 1 else big)[pages].reshape(256, LAT)
            length = rowinfo[2, pl.ds(g * 8, 8)].reshape(group, 128)[:, :1]
            scores = lax.dot_general(q, k, NT, preferred_element_type=jnp.float32) * SCALE
            scores = jnp.where(same & (token < length), scores, MASKED)
            high_own = jnp.max(scores, axis=1, keepdims=True)
            raised = jnp.exp(scores - high_own)
            total_own = jnp.sum(raised, axis=1, keepdims=True)
            blend_own = jnp.dot(
                raised.astype(jnp.bfloat16), k[:, :KVL], preferred_element_type=jnp.float32
            )
            high_pre = stats[0, rows, :][:, :1]
            total_pre = stats[1, rows, :][:, :1]
            ceiling = jnp.maximum(high_pre, high_own)
            f = jnp.exp(high_pre - ceiling)
            h = jnp.exp(high_own - ceiling)
            mixed = (f * blend[rows, :] + h * blend_own) / (f * total_pre + h * total_own)
            for l in range(KVL // 128):
                merged[l, rows, :] = mixed[:, l * 128:(l + 1) * 128]
        mine = pl.ds(pl.multiple_of(z * CH, CH), CH)
        for h in range(HEADS):
            a = jnp.concatenate(
                [merged[l, pl.ds(h, CH, stride=HEADS), :] for l in range(KVL // 128)], axis=1
            ).astype(jnp.bfloat16)
            zb[n, mine, h * VH:(h + 1) * VH] = jnp.dot(
                a, vup_v[h], preferred_element_type=jnp.float32
            ).astype(jnp.bfloat16)

    def new_pool():
        def place(i, row):
            new[128 * row + i] = big[listed(8 + row, i, POOL + 2 * MOVES)]
            return row

        for n, (row, count) in enumerate(((0, 128), (1, POOL - 128))):
            lax.fori_loop(0, count, place, row, unroll=4)
            part = pl.ds(128 * row, count)
            loads[f"new{row}"] = pltpu.make_async_copy(new.at[part], pool_o.at[part], lsem.at[7 + n])
            loads[f"new{row}"].start()

    def heads(n):
        def block(o):
            return zb.at[n, pl.ds(pl.multiple_of(o * CH, CH), CH)]

        def half(o, i):
            return zb.at[n, pl.ds(pl.multiple_of(o * CH + i * (CH // 2), CH // 2), CH // 2)]

        base = Z0 + 8 * n
        low = [rem(z + NZ - s, NZ) for s in range(4)]
        high = [rem(z + s, NZ) for s in range(5)]
        if n < CHUNKS - 1:
            send(block(z), block(z), at_z(z + 2), base + 2)
            send(block(z), block(z), at_z(z - 2), base + 3)
        else:
            first = [remote(block(z), block(z), at_z(z + 2 * w), base + 2 + (1 - w) // 2) for w in (1, -1)]
            for copy in first:
                copy.start()
            for copy in first:
                copy.wait_send()
        send(block(z), block(z), at_z(z + 1), base)
        send(block(z), block(z), at_z(z - 1), base + 1)
        yield
        arrived(block(low[2]), base + 2)
        send(half(low[2], 0), half(low[2], 0), at_z(z + 2), base + 6)
        send(block(low[2]), block(low[2]), at_z(z + 1), base + 4)
        arrived(block(high[2]), base + 3)
        send(half(high[2], 1), half(high[2], 1), at_z(z - 2), base + 7)
        send(block(high[2]), block(high[2]), at_z(z - 1), base + 5)
        yield
        arrived(block(low[1]), base)
        arrived(block(high[1]), base + 1)
        arrived(block(low[3]), base + 4)
        arrived(block(high[3]), base + 5)
        arrived(half(high[4], 0), base + 6)
        arrived(half(high[4], 1), base + 7)
        yield

    def product(n):
        for i in range(2):
            sx[n, i] = lax.dot_general(
                zb[n], w_v[2 * (1 - c) + i], NT, preferred_element_type=jnp.float32
            ).astype(jnp.bfloat16)
            send(sx.at[n, i], rx.at[n, i], partner, CX + 2 * n + i)
        for i in range(2):
            own[n, i] = lax.dot_general(zb[n], w_v[2 * c + i], NT, preferred_element_type=jnp.float32)

    def sums(n):
        base = RS + 16 * n

        @pl.when(rem(x, 2) == 1)
        def _():
            rr[n, 4] = jnp.zeros((2, CH, COLS), jnp.bfloat16)

        for i in range(2):
            arrived(rx.at[n, i], CX + 2 * n + i)
            ss[n, i] = (own[n, i] + rx[n, i].astype(jnp.float32)).astype(jnp.bfloat16)
        mine = rem(x, 2)

        def rows_of(s):
            return pl.ds(pl.multiple_of(rem(y + s, NY) * CH, CH), CH)

        def deliver(s, i):
            return remote(
                ss.at[n, i, rows_of(s)], rr.at[n, s, mine], owner(c, i, s), base + 2 * s + i, base + 2 * s + mine
            )

        send(ss.at[n, 1, rows_of(4)], relay.at[n], at_y(y - 2), RL + n)
        for s, i in ((4, 0), (3, 0), (3, 1), (5, 0), (5, 1), (2, 0), (2, 1), (6, 0), (1, 0), (1, 1), (7, 0), (7, 1)):
            copy = deliver(s, i)
            copy.start()
            sent.append(copy)
        for i in range(2):
            pl.when(jnp.logical_not(itself(i)))(deliver(0, i).start)

            @pl.when(itself(i))
            def _():
                rr[n, 0, mine] = ss[n, i, rows_of(0), :]
        yield
        arrived(relay.at[n], RL + n)
        ss[n, 1, rows_of(6)] = (
            ss[n, 1, rows_of(6), :].astype(jnp.float32) + relay[n].astype(jnp.float32)
        ).astype(jnp.bfloat16)
        copy = deliver(6, 1)
        copy.start()
        sent.append(copy)
        yield
        for e in range(2):
            total = None
            for s in (0, 1, 7, 2, 3, 5, 4, 6):
                copy = remote(rr.at[n, s, e], rr.at[n, s, e], partner, base + 2 * s + e)
                if s == 0:
                    pl.when(jnp.logical_not(itself(e)))(copy.wait_recv)
                elif s == 4:
                    pl.when(mine == 0)(copy.wait_recv)
                else:
                    copy.wait_recv()
                part = rr[n, s, e].astype(jnp.float32)
                total = part if total is None else total + part
            red[e, n * CH:(n + 1) * CH] = total
        rows = pl.ds(0, CH)
        for i in range(2):
            copy = remote(ss.at[n, i, rows], ss.at[n, i, rows], partner, base + i)
            pl.when(jnp.logical_not(itself(i)))(copy.wait_send)
        yield

    def order_copies(act):
        mine = rem(x, 2)
        for a in range(4):
            for column in range(NX):
                to = (2 * a + c) * NX + column
                copy = remote(
                    order_v, order_r.at[mine], (to, y * 2 + final_core), OR + 4 * a + column, OR + mine
                )
                pl.when((z == y) & jnp.logical_not(diagonal & (to == d)))(functools.partial(act, copy))

    def order_send():
        order_copies(lambda copy: copy.start())

        @pl.when((z == y) & diagonal & (rem(z, 2) == c))
        def _():
            order_r[rem(x, 2)] = order_v[...]

    def order_wait():
        order_copies(lambda copy: copy.wait_send())
        for e in range(2):
            copy = remote(order_v, order_r.at[e], partner, OR + e)
            pl.when(jnp.logical_not(order_itself(e)))(copy.wait_recv)

    def finish():
        loads["res"].wait()
        for e in range(2):
            place = order_r[e][:, :REQ]
            rows = pl.ds(e * REQ, REQ)
            total = red[e]
            high = total.astype(jnp.bfloat16)
            low = (total - high.astype(jnp.float32)).astype(jnp.bfloat16)
            placed = jnp.dot(place, high, preferred_element_type=jnp.float32) + jnp.dot(
                place, low, preferred_element_type=jnp.float32
            )
            out_ref[rows, :] = (res_v[rows, :].astype(jnp.float32) + placed).astype(jnp.bfloat16)

    running = {"p": pages_out(), "w": weights(), "r": pages_ring()}
    for n in range(CHUNKS):
        running[f"h{n}"] = heads(n)
        running[f"s{n}"] = sums(n)
    for step in PLAN:
        if step in running:
            next(running[step])
        elif step == "o":
            order_send()
        elif step == "O":
            order_wait()
        elif step == "n":
            new_pool()
        else:
            {"a": prefix_part, "b": own_part, "m": product}[step[0]](int(step[1]))
    finish()
    for copy in sent:
        copy.wait_send()
    loads["new0"].wait()
    loads["new1"].wait()


PARTS = 4


def settle(pool_h, layer_h, pool_o, layer_o, pool_v, layer_v, sem):
    parts = [pl.ds(n * (POOL // PARTS), POOL // PARTS) for n in range(PARTS)]
    loads = [pltpu.make_async_copy(pool_h.at[part], pool_v.at[part], sem.at[n]) for n, part in enumerate(parts)]
    stores = [pltpu.make_async_copy(pool_v.at[part], pool_o.at[part], sem.at[PARTS + n]) for n, part in enumerate(parts)]
    load = pltpu.make_async_copy(layer_h, layer_v, sem.at[2 * PARTS])
    store = pltpu.make_async_copy(layer_v, layer_o, sem.at[2 * PARTS + 1])
    for copy in loads:
        copy.start()
    load.start()
    for n in range(PARTS):
        loads[n].wait()
        stores[n].start()
    load.wait()
    store.start()
    for copy in stores:
        copy.wait()
    store.wait()


def local(
    queries, page_pool, prefix_cache, page_table, lengths, prefix_id, prefix_len,
    move_list, value_up, output_weight, residual,
):
    pages = page_table.T
    moves = move_list.transpose(2, 0, 1)
    smem = pl.BlockSpec(memory_space=pltpu.SMEM)
    vmem = pl.BlockSpec(memory_space=pltpu.VMEM)
    hbm = pl.BlockSpec(memory_space=pl.ANY)
    bf, f32 = jnp.bfloat16, jnp.float32
    vm = pltpu.VMEM
    layer_out, new_pool = pl.pallas_call(
        fused,
        out_shape=(
            jax.ShapeDtypeStruct((2 * REQ, COLS), bf),
            jax.ShapeDtypeStruct((POOL, PAGE, LAT), bf),
        ),
        in_specs=[smem] * 4 + [vmem] * 2 + [hbm] * 6,
        out_specs=(vmem, hbm),
        scratch_shapes=[
            vm((REQ, HEADS, LAT), bf), vm((POOL + 2 * MOVES, PAGE, LAT), bf), vm((2, LAT, PLEN), bf),
            vm((HEADS, KVL, VH), bf), vm((NX, COLS, DEPTH), bf), vm((2 * REQ, COLS), bf),
            vm((REQ, 128), bf), vm((2, REQ, 128), bf),
            vm((16, 128), jnp.int32), pltpu.SMEM((16, 128), jnp.int32),
            vm((8, PAGE, LAT), bf), vm((128, PAGE, LAT), bf), vm((CH, HEADS, LAT), f32),
            vm((2 * CH, PAGE, LAT), bf), vm((3, CH, HEADS, 128), jnp.int32), vm((ROWS, KVL), f32),
            vm((2, ROWS, 128), f32), vm((KVL // 128, ROWS, 128), f32),
            vm((CHUNKS, NZ * CH, DEPTH), bf), vm((CHUNKS, 2, NZ * CH, COLS), bf),
            vm((CHUNKS, 2, NZ * CH, COLS), bf), vm((CHUNKS, 2, NZ * CH, COLS), f32),
            vm((CHUNKS, 2, NZ * CH, COLS), bf), vm((CHUNKS, NY, 2, CH, COLS), bf),
            vm((CHUNKS, CH, COLS), bf), vm((2, REQ, COLS), f32), vm((POOL, PAGE, LAT), bf),
            pltpu.SemaphoreType.DMA((9,)),
            pltpu.SemaphoreType.DMA((SEMS,)),
            pltpu.SemaphoreType.DMA((SEMS,)),
        ],
        compiler_params=pltpu.CompilerParams(
            collective_id=0, has_side_effects=True, vmem_limit_bytes=60 * 1024 * 1024
        ),
        name="attention_block",
    )(
        pages, prefix_id, lengths, prefix_len, pages, moves,
        queries, page_pool, prefix_cache.transpose(0, 2, 1), value_up, output_weight.T, residual,
    )
    new_pool, layer_out = pl.pallas_call(
        settle,
        out_shape=(jax.ShapeDtypeStruct(new_pool.shape, bf), jax.ShapeDtypeStruct(layer_out.shape, bf)),
        in_specs=[hbm] * 2,
        out_specs=(hbm, hbm),
        scratch_shapes=[
            vm(new_pool.shape, bf), vm(layer_out.shape, bf), pltpu.SemaphoreType.DMA((2 * PARTS + 2,))
        ],
        compiler_params=pltpu.CompilerParams(vmem_limit_bytes=60 * 1024 * 1024),
        name="settle",
    )(new_pool, layer_out)
    return (layer_out, new_pool)


def solution(mesh):
    in_specs = (
        P("dp", "tp", None),
        P("dp", None, None),
        P(),
        P("dp", None),
        P("dp"),
        P("dp"),
        P(),
        P("dp", None, None),
        P("tp", None, None),
        P("tp", "dp"),
        P("tp", "dp"),
    )
    out_specs = (P("tp", "dp"), P("dp", None, None))
    return jax.shard_map(local, mesh=mesh, in_specs=in_specs, out_specs=out_specs, check_vma=False)
```
